256 devices in a mesh: dom: 64 (over x_hi, y, z), sub: 4 (over x_lo, core).
Axes of the slice: x: 4 (x_hi: 2, x_lo: 2; x = x_hi * 2 + x_lo), y: 4, z: 8, core: 2. Of those that a mesh axis runs over, the one named last changes fastest.
Arguments:
- positions: float32 [64, 4, 3, 256], P('dom', 'sub'), may hold values from 0 to 4
- species: int32 [64, 4, 256], P('dom', 'sub'), may hold values from 0 to 9
- boundary: int32 [64, 4, 128], P('dom', 'sub'), may hold values from 0 to 255, as said below
- neighbours: int32 [64, 4, 16, 256], P('dom', 'sub'), may hold values from 0 to 1408, as said below
- embed: bfloat16 [10, 128], replicated, may hold values from -4 to 4
- rad1_in: bfloat16 [8, 64], replicated, may hold values from -4 to 4
- rad1_out: bfloat16 [64, 384], replicated, may hold values from -0.75 to 0.75
- self1: bfloat16 [128, 128], replicated, may hold values from -0.5 to 0.5
- mix1: bfloat16 [384, 128], replicated, may hold values from -0.3125 to 0.3125
- gate1: bfloat16 [128, 128], replicated, may hold values from -0.5 to 0.5
- read1: float32 [128], replicated, may hold values from -0.5 to 0.5
- rad2_in: bfloat16 [8, 64], replicated, may hold values from -4 to 4
- rad2_out: bfloat16 [64, 512], replicated, may hold values from -0.75 to 0.75
- self2: bfloat16 [128, 128], replicated, may hold values from -0.5 to 0.5
- mix2: bfloat16 [384, 128], replicated, may hold values from -0.3125 to 0.3125
- out_in: bfloat16 [128, 16], replicated, may hold values from -0.5 to 0.5
- out_last: float32 [16], replicated, may hold values from -1.5 to 1.5
Outputs:
- energies: float32 [64, 4, 256], P('dom', 'sub')
- forces: float32 [64, 4, 3, 256], P('dom', 'sub')
The draws below stay inside these ranges and needn't reach their ends.
Inputs may be any that keep to these rules, and one draw needn't show every extreme that they name: `neighbours`: on one device, entry (k, i) names neighbour k of own atom i: v < 256 is own atom v, never i; 256 + 128 * (3 a + b) + t with (a, b) != (1, 1) is entry t of boundary on the device a - 1 steps along dom and b - 1 along sub (periodic); 1408 is an empty slot; live slots come first. `boundary`: the entries of one device are distinct.
All inputs are finite; a program needn't handle non-finite values.
Results may differ from the reference program's by a relative error of at most 0.00035.
Values sent between devices are 32-bit elements; how exact they have to be, the bound alone decides.
A program may use at most 192 MiB of HBM per device.

```python
import math
import jax
import jax.numpy as jnp
from jax import lax

C = 128
RADIAL = 64
BASIS = 8
OUTH = 16
KINDS = 10
NEIGH = 16
ATOM_DEV = 256
BOUND_DEV = 128
N_DOM = 64
N_SUB = 4


def draw_boundary(key, part):
    key = jax.random.fold_in(key, 7)
    scores = jax.random.randint(key, (N_DOM, N_SUB, ATOM_DEV), 0, 2 ** 20) * ATOM_DEV
    scores = scores + jnp.arange(ATOM_DEV, dtype=jnp.int32)[None, None, :]
    ordered = jnp.argsort(scores, axis=-1, stable=True)
    return ordered[..., :BOUND_DEV].astype(jnp.int32)


def draw_neighbours(key, part):
    key = jax.random.fold_in(key, 11)
    keys = jax.random.split(key, 7)
    shape = (N_DOM, N_SUB, NEIGH, ATOM_DEV)
    dense = jax.random.randint(keys[0], (N_DOM, N_SUB, 1, 1), 0, 2)
    sparse_count = jax.random.randint(keys[1], (N_DOM, N_SUB, 1, ATOM_DEV), NEIGH // 4, NEIGH // 2 + 1)
    dense_count = jax.random.randint(keys[2], (N_DOM, N_SUB, 1, ATOM_DEV), NEIGH // 2, NEIGH + 1)
    live_count = jnp.where(dense == 1, dense_count, sparse_count)
    slots = jnp.arange(NEIGH, dtype=jnp.int32)[None, None, :, None]
    atom_ids = jnp.arange(ATOM_DEV, dtype=jnp.int32)[None, None, None, :]
    own_pick = (atom_ids + 1 + jax.random.randint(keys[3], shape, 0, ATOM_DEV - 1)) % ATOM_DEV
    block = jax.random.randint(keys[4], shape, 0, 8)
    block = block + (block >= 4).astype(jnp.int32)
    ghost_pick = ATOM_DEV + block * BOUND_DEV + jax.random.randint(keys[5], shape, 0, BOUND_DEV)
    side = jax.random.randint(keys[6], shape, 0, 2)
    picked = jnp.where(side == 1, own_pick, ghost_pick)
    return jnp.where(slots < live_count, picked, ATOM_DEV + 9 * BOUND_DEV).astype(jnp.int32)


def touch_ends(values, stream_key, low, high):
    longest = values.shape.index(max(values.shape))
    spots = []
    for shift in (0, 1):
        where = [jax.random.randint(jax.random.fold_in(stream_key, axis), (), 0, length) for axis, length in enumerate(values.shape)]
        where[longest] = (where[longest] + shift) % values.shape[longest]
        spots.append(tuple(where))
    return values.at[spots[0]].set(low).at[spots[1]].set(high)


def shard_levels(own_key, dims, cuts, low, largest):
    def one(dim, shards_of):
        draws = jax.random.uniform(jax.random.fold_in(jax.random.fold_in(own_key, 6), dim), (shards_of,), jnp.float32, low / len(cuts), largest / len(cuts))
        return jnp.repeat(jnp.exp(draws), dims[dim] // shards_of).reshape((-1,) + (1,) * (len(dims) - dim - 1))

    factor_of = one(*cuts[0])
    for cut in cuts[1:]:
        factor_of = factor_of * one(*cut)
    return factor_of


def bell_draw(key, shape, spread, limit, held_as=jnp.bfloat16):
    return jnp.clip(spread * jax.random.normal(key, shape, jnp.float32), -limit, limit).astype(held_as)


def setup_inputs(seed: int = 0) -> dict:
    seeds = jax.random.split(jax.random.key(seed), 18)
    positions = jnp.clip(4.0 * jax.random.uniform(seeds[0], (N_DOM, N_SUB, 3, ATOM_DEV), jnp.float32) ** shard_levels(seeds[0], (N_DOM, N_SUB, 3, ATOM_DEV), ((0, 64), (1, 4)), -0.2, 0.2), 0.0, 4.0)
    species = touch_ends(jax.random.randint(seeds[1], (N_DOM, N_SUB, ATOM_DEV), 0, KINDS), jax.random.fold_in(seeds[1], 1), 0, KINDS - 1).astype(jnp.int32)
    boundary = draw_boundary(jax.random.fold_in(seeds[17], 71), 0)
    neighbours = draw_neighbours(jax.random.fold_in(seeds[17], 71), 0)
    embed = bell_draw(seeds[4], (KINDS, C), 1.0, 4.0)
    rad1_in = bell_draw(seeds[5], (BASIS, RADIAL), 1.0, 4.0)
    rad1_out = bell_draw(seeds[6], (RADIAL, 3 * C), RADIAL ** -0.5, 0.75)
    self1 = bell_draw(seeds[7], (C, C), C ** -0.5, 0.5)
    mix1 = bell_draw(seeds[8], (3 * C, C), (3 * C) ** -0.5, 0.3125)
    gate1 = bell_draw(seeds[9], (C, C), C ** -0.5, 0.5)
    read1 = bell_draw(seeds[10], (C,), C ** -0.5, 0.5, jnp.float32)
    rad2_in = bell_draw(seeds[11], (BASIS, RADIAL), 1.0, 4.0)
    rad2_out = bell_draw(seeds[12], (RADIAL, 4 * C), RADIAL ** -0.5, 0.75)
    self2 = bell_draw(seeds[13], (C, C), C ** -0.5, 0.5)
    mix2 = bell_draw(seeds[14], (3 * C, C), (3 * C) ** -0.5, 0.3125)
    out_in = bell_draw(seeds[15], (C, OUTH), C ** -0.5, 0.5)
    out_last = bell_draw(seeds[16], (OUTH,), OUTH ** -0.5, 1.5, jnp.float32)
    return dict(positions=positions, species=species, boundary=boundary, neighbours=neighbours, embed=embed, rad1_in=rad1_in, rad1_out=rad1_out, self1=self1, mix1=mix1, gate1=gate1, read1=read1, rad2_in=rad2_in, rad2_out=rad2_out, self2=self2, mix2=mix2, out_in=out_in, out_last=out_last)


CUTOFF = 5.0

def project(weight, inputs):
    return jnp.dot(weight.astype(jnp.float32).T, inputs, precision=lax.Precision.HIGHEST)

def edge_terms(pos_ext, listed, basis_count):
    atom_count = listed.shape[1]
    empty_slot = pos_ext.shape[1] - 1
    present = (listed < empty_slot).astype(jnp.float32)
    direction = (pos_ext[:, listed] - pos_ext[:, :atom_count][:, None, :]) / CUTOFF
    radius2 = lax.optimization_barrier(jnp.sum(direction * direction, axis=0))
    envelope = jnp.square(jnp.maximum(1.0 - radius2, 0.0)) * present
    orders = jnp.arange(basis_count).astype(jnp.float32)[:, None, None]
    basis = envelope[None] * jnp.cos(math.pi * orders * radius2[None])
    along_x, along_y, along_z = (direction[0], direction[1], direction[2])
    harmonics = jnp.stack([jnp.ones_like(along_x), 1.7 * along_x, 1.7 * along_y, 1.7 * along_z, 3.9 * along_x * along_y, 3.9 * along_y * along_z, 1.1 * (3.0 * along_z * along_z - radius2), 3.9 * along_x * along_z, 1.95 * (along_x * along_x - along_y * along_y)])
    return (basis, harmonics)

def radial(basis, weight_in, weight_out, part_count):
    basis_count, slots, atom_count = basis.shape
    hidden = jax.nn.silu(project(weight_in, basis.reshape(basis_count, slots * atom_count)))
    result = project(weight_out, hidden)
    return result.reshape(part_count, -1, slots, atom_count)

def aggregate(weight_set, harmonics, source):
    factor = weight_set.shape[2] ** (-0.5)
    monopole = lax.optimization_barrier(jnp.sum(weight_set[0] * source * harmonics[0][None], axis=1))[None]
    dipole = lax.optimization_barrier(jnp.sum((weight_set[1] * source)[None] * harmonics[1:4][:, None], axis=2))
    quadrupole = lax.optimization_barrier(jnp.sum((weight_set[2] * source)[None] * harmonics[4:9][:, None], axis=2))
    return jnp.concatenate([monopole, dipole, quadrupole], axis=0) * factor

def invariants(amplitudes):
    return jnp.concatenate([amplitudes[0], lax.optimization_barrier(jnp.sum(amplitudes[1:4] ** 2, axis=0)), lax.optimization_barrier(jnp.sum(amplitudes[4:9] ** 2, axis=0))], axis=0)

def layer_one(pos_ext, species_ext, listed, embed, weight_in, weight_out, self_weight, mix_weight, gate_weight, read_weight):
    atom_count = listed.shape[1]
    basis, harmonics = edge_terms(pos_ext, listed, weight_in.shape[0])
    onehot = (species_ext[None, :] == jnp.arange(embed.shape[0], dtype=jnp.int32)[:, None]).astype(jnp.float32)
    node_feat = project(embed, onehot)
    amplitudes = aggregate(radial(basis, weight_in, weight_out, 3), harmonics, node_feat[:, listed])
    scalars = project(self_weight, node_feat[:, :atom_count]) + project(mix_weight, invariants(amplitudes))
    gating = jax.nn.sigmoid(project(gate_weight, scalars))
    vectors = amplitudes[1:4] * gating[None]
    energy = jnp.dot(read_weight.astype(jnp.float32), scalars, precision=lax.Precision.HIGHEST)
    return (scalars, vectors, energy)

def layer_two(pos_ext, scalars_ext, vectors_ext, listed, weight_in, weight_out, self_weight, mix_weight, out_in, out_last):
    atom_count = listed.shape[1]
    basis, harmonics = edge_terms(pos_ext, listed, weight_in.shape[0])
    weight_set = radial(basis, weight_in, weight_out, 4)
    amplitudes = aggregate(weight_set[:3], harmonics, scalars_ext[:, listed])
    factor = listed.shape[0] ** (-0.5)
    carried = lax.optimization_barrier(jnp.sum(weight_set[3][None] * vectors_ext[:, :, listed], axis=2)) * factor
    amplitudes = jnp.concatenate([amplitudes[0:1], amplitudes[1:4] + carried, amplitudes[4:9]], axis=0)
    scalars_two = project(self_weight, scalars_ext[:, :atom_count]) + project(mix_weight, invariants(amplitudes))
    hidden = jax.nn.silu(project(out_in, scalars_two))
    return jnp.dot(out_last.astype(jnp.float32), hidden, precision=lax.Precision.HIGHEST)

def reference(positions, species, boundary, neighbours, embed, rad1_in, rad1_out, self1, mix1, gate1, read1, rad2_in, rad2_out, self2, mix2, out_in, out_last):
    device_count = N_DOM * N_SUB

    def extend(table, device):
        dom_index = device // N_SUB
        sub_index = device % N_SUB
        own_part = table[dom_index, sub_index]
        blocks = [own_part]
        for row_off in range(3):
            for col_off in range(3):
                dom_near = (dom_index + row_off - 1) % N_DOM
                sub_near = (sub_index + col_off - 1) % N_SUB
                blocks.append(jnp.take(table[dom_near, sub_near], boundary[dom_near, sub_near], axis=-1))
        blocks.append(jnp.zeros(own_part.shape[:-1] + (1,), own_part.dtype))
        return jnp.concatenate(blocks, axis=-1)

    def total_energy(coords):

        def first_layer(device):
            listed = neighbours[device // N_SUB, device % N_SUB]
            return layer_one(extend(coords, device), extend(species, device), listed, embed, rad1_in, rad1_out, self1, mix1, gate1, read1)
        devices = jnp.arange(device_count, dtype=jnp.int32)
        scalars, vectors, energy_one = lax.map(jax.checkpoint(first_layer), devices)
        scalars_grid = scalars.reshape((N_DOM, N_SUB) + scalars.shape[1:])
        vectors_grid = vectors.reshape((N_DOM, N_SUB) + vectors.shape[1:])

        def second_layer(device):
            listed = neighbours[device // N_SUB, device % N_SUB]
            return layer_two(extend(coords, device), extend(scalars_grid, device), extend(vectors_grid, device), listed, rad2_in, rad2_out, self2, mix2, out_in, out_last)
        energy_two = lax.map(jax.checkpoint(second_layer), devices)
        energies = (energy_one + energy_two).reshape(N_DOM, N_SUB, -1)
        return (jnp.sum(energies), energies)
    gradients, energies = jax.grad(total_energy, has_aux=True)(positions)
    return (energies, -gradients)
```

```python
import math

import jax
import jax.numpy as jnp
from jax import lax
from jax.experimental import pallas as pl
from jax.experimental.pallas import tpu as pltpu
from jax.sharding import PartitionSpec as P

CUTOFF = 5.0
MESH = pl.DeviceIdType.MESH
F32 = jnp.float32
BF16 = jnp.bfloat16
C = 128
SLOTS = 16
ATOMS = 256
BORDER = 128
EDGES = SLOTS * ATOMS
EXT = ATOMS + 8 * BORDER
SIDES = [(a, b) for a in (-1, 0, 1) for b in (-1, 0, 1) if (a, b) != (0, 0)]
HALF = SLOTS ** (-0.5)


def dot(a, b):
    return jnp.dot(a, b, preferred_element_type=F32)


def dot_nt(a, b):
    return lax.dot_general(a, b, (((1,), (1,)), ((), ())), preferred_element_type=F32)


def split(x):
    high = x.astype(BF16)
    return high, (x - high.astype(F32)).astype(BF16)


def stack2(x):
    high = x.astype(BF16).astype(F32)
    return jnp.concatenate([high, x - high], axis=0).astype(BF16)


def stack4(x):
    high = x.astype(BF16).astype(F32)
    rest = x - high
    mid = rest.astype(BF16).astype(F32)
    return jnp.concatenate([high, mid, rest - mid, jnp.zeros_like(x)], axis=0).astype(BF16)


def turned(weight, copies=1):
    tall = weight.astype(F32)
    if copies > 1:
        tall = jnp.concatenate([tall] * copies, axis=0)
    return tall.T.astype(BF16)


def doubled(weight):
    return jnp.concatenate([weight, weight], axis=1)


def sine(z):
    z2 = z * z
    out = 1.0 / 6227020800.0
    for coefficient in (-1.0 / 39916800.0, 1.0 / 362880.0, -1.0 / 5040.0, 1.0 / 120.0, -1.0 / 6.0, 1.0):
        out = out * z2 + coefficient
    return out * z


def cosine(z):
    z2 = z * z
    out = 1.0 / 479001600.0 - z2 * (1.0 / 87178291200.0)
    for coefficient in (-1.0 / 3628800.0, 1.0 / 40320.0, -1.0 / 720.0, 1.0 / 24.0, -0.5, 1.0):
        out = out * z2 + coefficient
    return out


def sigmoid(x):
    return 1.0 / (1.0 + jnp.exp(-x))


def lanes(k, width=ATOMS):
    return pl.ds(pl.multiple_of(k * width, width), width)


def kernel(
    shape_of_mesh,
    pos_ref,
    spec_ref,
    bound_ref,
    neigh_ref,
    embed_ref,
    rad1_in_ref,
    rad1_out_ref,
    self1_ref,
    mix1_ref,
    gate1_ref,
    read1_ref,
    rad2_in_ref,
    rad2_out_ref,
    self2_ref,
    mix2_ref,
    out_in_ref,
    out_last_ref,
    energy_ref,
    force_ref,
    hot,
    listed,
    rad1,
    rad2,
    src1,
    src2,
    terms,
    slope1,
    slope2,
    basis,
    basis_slope,
    shift,
    harm,
    d_harm,
    d_radius,
    amps1,
    amps2,
    back,
    feats,
    own_grad,
    out_feat,
    got_feat,
    out_grad,
    got_grad,
    out_pos,
    got_pos,
    out_force,
    got_force,
    send_sem,
    recv_sem,
):
    n_dom, n_sub = shape_of_mesh
    dom = lax.axis_index("dom")
    sub = lax.axis_index("sub")

    def device(a, b):
        return (lax.rem(dom + a + n_dom, n_dom), lax.rem(sub + b + n_sub, n_sub))

    barrier = pltpu.get_barrier_semaphore()
    for a, b in SIDES:
        pl.semaphore_signal(barrier, inc=1, device_id=device(a, b), device_id_type=MESH)

    def transfer(phase, source, target, o, sign):
        a, b = SIDES[o]
        return pltpu.make_async_remote_copy(
            src_ref=source,
            dst_ref=target,
            send_sem=send_sem.at[phase, o],
            recv_sem=recv_sem.at[phase, o],
            device_id=device(sign * a, sign * b),
            device_id_type=MESH,
        )

    own_rows = jnp.concatenate(
        [pos_ref[0, 0], spec_ref[0].astype(F32), jnp.zeros((4, ATOMS), F32)], axis=0
    )
    border_hot = (
        lax.broadcasted_iota(jnp.int32, (ATOMS, BORDER), 0) == bound_ref[0]
    ).astype(F32).astype(BF16)
    picked = dot(stack4(own_rows), border_hot)
    out_pos[...] = picked[0:8] + picked[8:16] + picked[16:24]
    pl.semaphore_wait(barrier, 8)
    sent_pos = [transfer(0, out_pos, got_pos.at[o], o, -1) for o in range(8)]
    for copy in sent_pos:
        copy.start()

    for k in range(SLOTS):
        row = neigh_ref[0, 0, k : k + 1, :]
        listed[:, k * ATOMS : (k + 1) * ATOMS] = jnp.where(
            row >= ATOMS + 5 * BORDER, row - BORDER, row
        )

    def build(k, carry):
        at = lanes(k)
        ids = lax.broadcasted_iota(jnp.int32, (EXT, ATOMS), 0)
        hot[:, at] = jnp.where(ids == listed[:, at], 1.0, 0.0).astype(BF16)
        return carry

    lax.fori_loop(0, SLOTS, build, 0)

    rad1_in_t = turned(rad1_in_ref[...], 2)
    rad1_out_t = turned(rad1_out_ref[...], 2)
    rad2_in_t = turned(rad2_in_ref[...], 2)
    rad2_out_t = turned(rad2_out_ref[...], 2)
    embed_t = turned(
        jnp.concatenate([embed_ref[...].astype(F32), jnp.zeros((6, C), F32)], axis=0)
    )

    for copy in sent_pos:
        copy.wait()
    table = stack4(jnp.concatenate([own_rows] + [got_pos[o] for o in range(8)], axis=1))

    def geometry(g, carry):
        at = lanes(g, 1024)
        found = dot(table, hot[:, at])
        there = found[0:8] + found[8:16] + found[16:24]
        here = jnp.concatenate([own_rows] * 4, axis=1)
        u = (there - here) * (1.0 / CUTOFF)
        shift[:, at] = u
        ux, uy, uz = u[0:1], u[1:2], u[2:3]
        r2 = ux * ux + uy * uy + uz * uz
        present = jnp.where(listed[:, at] < EXT, 1.0, 0.0)
        room = jnp.maximum(1.0 - r2, 0.0) * present
        orders = lax.broadcasted_iota(jnp.int32, (8, 1024), 0).astype(F32)
        turns = orders * jnp.minimum(r2, 1.0)
        turns = turns - 2.0 * jnp.floor(0.5 * turns + 0.5)
        z = (0.5 * math.pi) * turns
        sz, cz = sine(z), cosine(z)
        cos_n = 1.0 - 2.0 * sz * sz
        sin_n = 2.0 * sz * cz
        envelope = room * room
        base = envelope * cos_n
        basis[:, at] = base
        basis_slope[:, at] = -2.0 * room * cos_n - (math.pi * orders) * (envelope * sin_n)
        harm[0:1, at] = 1.7 * ux
        harm[1:2, at] = 1.7 * uy
        harm[2:3, at] = 1.7 * uz
        harm[3:4, at] = 3.9 * ux * uy
        harm[4:5, at] = 3.9 * uy * uz
        harm[5:6, at] = 1.1 * (3.0 * uz * uz - r2)
        harm[6:7, at] = 3.9 * ux * uz
        harm[7:8, at] = 1.95 * (ux * ux - uy * uy)
        kinds = lax.broadcasted_iota(jnp.int32, (16, 1024), 0).astype(F32)
        src1[:, at] = dot(embed_t, jnp.where(kinds == there[3:4], 1.0, 0.0).astype(BF16))
        radial(base, rad1_in_t, rad1_out_t, slope1, rad1, at)
        return carry

    def radial(base, in_t, out_t, slope, rad, at):
        pre = dot(in_t, stack2(base))
        gate = sigmoid(pre)
        slope[:, at] = gate * (1.0 + pre * (1.0 - gate))
        rad[:, at] = dot(out_t, stack2(pre * gate))

    lax.fori_loop(0, 4, geometry, 0)

    def aggregate(rad, src, amps, vectors):
        def step(t, carry):
            r = t * 8
            total = [jnp.zeros((8, ATOMS), F32) for _ in range(9)]
            for k in range(SLOTS):
                at = slice(k * ATOMS, (k + 1) * ATOMS)

                def rows(ref, block):
                    return ref[pl.ds(pl.multiple_of(block * C + r, 8), 8), at]

                s = rows(src, 0)
                total[0] += rows(rad, 0) * s
                p1 = rows(rad, 1) * s
                p2 = rows(rad, 2) * s
                for m in range(3):
                    total[1 + m] += p1 * harm[m : m + 1, at]
                for m in range(3, 8):
                    total[1 + m] += p2 * harm[m : m + 1, at]
                if vectors:
                    r3 = rows(rad, 3)
                    for m in range(3):
                        total[1 + m] += r3 * rows(src, 1 + m)
            for m in range(9):
                amps[pl.ds(pl.multiple_of(m * C + r, 8), 8), :] = total[m] * HALF
            return carry

        lax.fori_loop(0, C // 8, step, 0)

    def invariants(amps):
        a = [amps[m * C : (m + 1) * C, :] for m in range(9)]
        dipole = a[1] * a[1] + a[2] * a[2] + a[3] * a[3]
        quadrupole = a[4] * a[4] + a[5] * a[5] + a[6] * a[6] + a[7] * a[7] + a[8] * a[8]
        return jnp.concatenate([a[0], dipole, quadrupole], axis=0)

    aggregate(rad1, src1, amps1, False)
    own_kinds = lax.broadcasted_iota(jnp.int32, (16, ATOMS), 0)
    own_node = dot(embed_t, jnp.where(own_kinds == spec_ref[0], 1.0, 0.0).astype(BF16))
    scalars = dot(turned(self1_ref[...]), own_node.astype(BF16)) + dot(
        turned(mix1_ref[...], 2), stack2(invariants(amps1))
    )
    gating = sigmoid(dot(turned(gate1_ref[...], 2), stack2(scalars)))
    read = jnp.concatenate([jnp.broadcast_to(read1_ref[...], (C, C)).T] * 2, axis=1)
    energy_one = jnp.sum(read * scalars, axis=0, keepdims=True)
    own_feat = jnp.concatenate(
        [scalars] + [amps1[m * C : (m + 1) * C, :] * gating for m in range(1, 4)], axis=0
    )
    own_terms = stack2(own_feat)
    feats[:, 0:ATOMS] = own_terms
    picked_feat = dot(own_terms, border_hot)
    out_feat[...] = picked_feat[0:512] + picked_feat[512:1024]
    sent_feat = [transfer(1, out_feat, got_feat.at[o], o, -1) for o in range(8)]
    for copy in sent_feat:
        copy.start()

    def second_radial(g, carry):
        at = lanes(g, 1024)
        radial(basis[:, at], rad2_in_t, rad2_out_t, slope2, rad2, at)
        return carry

    lax.fori_loop(0, 4, second_radial, 0)

    for o in range(8):
        sent_feat[o].wait()
        feats[:, ATOMS + o * BORDER : ATOMS + (o + 1) * BORDER] = stack2(got_feat[o])

    def gather(k, carry):
        at = lanes(k)
        found = dot(feats[...], hot[:, at])
        src2[:, at] = found[0:512] + found[512:1024]
        return carry

    lax.fori_loop(0, SLOTS, gather, 0)
    aggregate(rad2, src2, amps2, True)
    scalars_two = dot(turned(self2_ref[...], 2), stack2(scalars)) + dot(
        turned(mix2_ref[...], 2), stack2(invariants(amps2))
    )
    pre = dot(turned(out_in_ref[...], 2), stack2(scalars_two))
    gate = sigmoid(pre)
    last = jnp.concatenate([jnp.broadcast_to(out_last_ref[...], (C, 16)).T] * 2, axis=1)
    energy_two = jnp.sum(last * (pre * gate), axis=0, keepdims=True)
    energy_ref[0] = energy_one + energy_two

    d_pre = last * (gate * (1.0 + pre * (1.0 - gate)))
    d_pre_high, d_pre_low = split(d_pre)
    d_two = dot(out_in_ref[...], d_pre_high) + dot(out_in_ref[...], d_pre_low)
    d_two_terms = stack2(d_two)
    d_self = dot(doubled(self2_ref[...]), d_two_terms)
    d_inv = dot(doubled(mix2_ref[...]), d_two_terms)

    def to_back(amps, d_inv, extra):
        back[0:C, :] = d_inv[0:C] * HALF
        for m in range(1, 9):
            block = d_inv[C : 2 * C] if m < 4 else d_inv[2 * C : 3 * C]
            value = 2.0 * amps[m * C : (m + 1) * C, :] * block
            if extra is not None and m < 4:
                value = value + extra[m - 1]
            back[m * C : (m + 1) * C, :] = value * HALF

    to_back(amps2, d_inv, None)

    def source_grads(k, carry):
        at = lanes(k)
        for t in range(C // 16):
            b = [back[m * C + t * 16 : m * C + t * 16 + 16, :] for m in range(9)]
            r0, r1, r2, r3 = [rad2[l * C + t * 16 : l * C + t * 16 + 16, at] for l in range(4)]
            t1 = harm[0:1, at] * b[1] + harm[1:2, at] * b[2] + harm[2:3, at] * b[3]
            t2 = harm[3:4, at] * b[4]
            for m in range(4, 8):
                t2 = t2 + harm[m : m + 1, at] * b[m + 1]
            grads = [r0 * b[0] + r1 * t1 + r2 * t2] + [r3 * b[m] for m in range(1, 4)]
            for l in range(4):
                high, low = split(grads[l])
                terms[l * C + t * 16 : l * C + t * 16 + 16, at] = high
                terms[512 + l * C + t * 16 : 512 + l * C + t * 16 + 16, at] = low
        return carry

    lax.fori_loop(0, SLOTS, source_grads, 0)

    sent_grad = [transfer(2, out_grad.at[o], got_grad.at[o], o, 1) for o in range(8)]
    for n in (1, 2, 3, 4, 0):
        summed = dot_nt(terms[...], hot[n * 256 : (n + 1) * 256, :])
        summed = summed[0:512] + summed[512:1024]
        if n == 0:
            own_grad[...] = summed
        else:
            for o in (2 * n - 2, 2 * n - 1):
                out_grad[o] = summed[:, (o % 2) * BORDER : (o % 2 + 1) * BORDER]
                sent_grad[o].start()

    def radial_grads(rad, src, slope, in_ref, out_ref, blocks, first):
        out_pair = doubled(out_ref[...])

        def step(k, carry):
            at = lanes(k)
            total = [jnp.zeros((8, ATOMS), F32) for _ in range(8)]
            for t in range(C // 16):
                b = [back[m * C + t * 16 : m * C + t * 16 + 16, :] for m in range(9)]
                t1 = harm[0:1, at] * b[1] + harm[1:2, at] * b[2] + harm[2:3, at] * b[3]
                t2 = harm[3:4, at] * b[4]
                for m in range(4, 8):
                    t2 = t2 + harm[m : m + 1, at] * b[m + 1]
                s = src[t * 16 : t * 16 + 16, at]
                grads = [s * b[0], s * t1, s * t2]
                if blocks == 4:
                    v = [src[l * C + t * 16 : l * C + t * 16 + 16, at] for l in range(1, 4)]
                    grads.append(v[0] * b[1] + v[1] * b[2] + v[2] * b[3])
                for l in range(blocks):
                    high, low = split(grads[l])
                    terms[l * C + t * 16 : l * C + t * 16 + 16, at] = high
                    terms[
                        (blocks + l) * C + t * 16 : (blocks + l) * C + t * 16 + 16, at
                    ] = low
                p1 = rad[C + t * 16 : C + t * 16 + 16, at] * s
                p2 = rad[2 * C + t * 16 : 2 * C + t * 16 + 16, at] * s
                for m in range(8):
                    product = (p1 if m < 3 else p2) * b[m + 1]
                    total[m] += product[0:8] + product[8:16]
            for m in range(8):
                value = jnp.sum(total[m], axis=0, keepdims=True)
                if not first:
                    value = value + d_harm[m : m + 1, at]
                d_harm[m : m + 1, at] = value
            return carry

        lax.fori_loop(0, SLOTS, step, 0)

        def tail(g, carry):
            at = lanes(g, 1024)
            d_hidden = dot(out_pair, terms[0 : 2 * blocks * C, at]) * slope[:, at]
            high, low = split(d_hidden)
            d_basis = dot(in_ref[...], high) + dot(in_ref[...], low)
            value = jnp.sum(d_basis * basis_slope[:, at], axis=0, keepdims=True)
            if not first:
                value = value + d_radius[:, at]
            d_radius[:, at] = value
            return carry

        lax.fori_loop(0, 4, tail, 0)

    radial_grads(rad2, src2, slope2, rad2_in_ref, rad2_out_ref, 4, True)

    for copy in sent_grad:
        copy.wait()
    returned = got_grad[0]
    for o in range(1, 8):
        returned = returned + got_grad[o]
    placed = dot_nt(stack2(returned), border_hot)
    d_feat = own_grad[...] + placed[0:512] + placed[512:1024]
    d_vec = [d_feat[m * C : (m + 1) * C] for m in range(1, 4)]
    d_gate = (
        d_vec[0] * amps1[C : 2 * C, :]
        + d_vec[1] * amps1[2 * C : 3 * C, :]
        + d_vec[2] * amps1[3 * C : 4 * C, :]
    ) * (gating * (1.0 - gating))
    d_scalars = d_feat[0:C] + d_self + read + dot(doubled(gate1_ref[...]), stack2(d_gate))
    d_inv_one = dot(doubled(mix1_ref[...]), stack2(d_scalars))
    to_back(amps1, d_inv_one, [d * gating for d in d_vec])
    radial_grads(rad1, src1, slope1, rad1_in_ref, rad1_out_ref, 3, False)

    def to_shift(g, carry):
        at = lanes(g, 1024)
        ux, uy, uz = [shift[m : m + 1, at] for m in range(3)]
        d = [d_harm[m : m + 1, at] for m in range(8)]
        dr = 2.0 * (d_radius[:, at] - 1.1 * d[5])
        basis[0:1, at] = (
            1.7 * d[0] + 3.9 * (uy * d[3] + uz * d[6] + ux * d[7]) + ux * dr
        ) * (1.0 / CUTOFF)
        basis[1:2, at] = (
            1.7 * d[1] + 3.9 * (ux * d[3] + uz * d[4] - uy * d[7]) + uy * dr
        ) * (1.0 / CUTOFF)
        basis[2:3, at] = (
            1.7 * d[2] + 3.9 * (uy * d[4] + ux * d[6]) + uz * (6.6 * d[5] + dr)
        ) * (1.0 / CUTOFF)
        basis[3:8, at] = jnp.zeros((5, 1024), F32)
        return carry

    lax.fori_loop(0, 4, to_shift, 0)
    d_edges = stack4(basis[...])
    sent_force = [transfer(3, out_force.at[o], got_force.at[o], o, 1) for o in range(8)]
    own_force = None
    for n in (1, 2, 3, 4, 0):
        summed = dot_nt(d_edges, hot[n * 256 : (n + 1) * 256, :])
        summed = summed[0:8] + summed[8:16] + summed[16:24]
        if n == 0:
            own_force = summed
        else:
            for o in (2 * n - 2, 2 * n - 1):
                out_force[o] = summed[:, (o % 2) * BORDER : (o % 2 + 1) * BORDER]
                sent_force[o].start()
    for k in range(SLOTS):
        own_force = own_force - basis[:, k * ATOMS : (k + 1) * ATOMS]
    for copy in sent_force:
        copy.wait()
    returned = got_force[0]
    for o in range(1, 8):
        returned = returned + got_force[o]
    placed = dot_nt(stack4(returned), border_hot)
    own_force = own_force + placed[0:8] + placed[8:16] + placed[16:24]
    force_ref[0, 0] = -own_force[0:3]


def solution(mesh):
    shape_of_mesh = (mesh.shape["dom"], mesh.shape["sub"])

    def vmem(*shape, dtype=F32):
        return pltpu.VMEM(shape, dtype)

    def body(*args):
        args = list(args)
        args[10] = args[10].reshape(1, C)
        args[16] = args[16].reshape(1, 16)

        def run(*refs):
            kernel(shape_of_mesh, *refs)

        return pl.pallas_call(
            run,
            out_shape=(
                jax.ShapeDtypeStruct((1, 1, ATOMS), F32),
                jax.ShapeDtypeStruct((1, 1, 3, ATOMS), F32),
            ),
            in_specs=[pl.BlockSpec(memory_space=pltpu.VMEM)] * 17,
            out_specs=[pl.BlockSpec(memory_space=pltpu.VMEM)] * 2,
            scratch_shapes=[
                vmem(EXT, EDGES, dtype=BF16),
                vmem(1, EDGES, dtype=jnp.int32),
                vmem(3 * C, EDGES),
                vmem(4 * C, EDGES),
                vmem(C, EDGES),
                vmem(4 * C, EDGES),
                vmem(8 * C, EDGES, dtype=BF16),
                vmem(64, EDGES),
                vmem(64, EDGES),
                vmem(8, EDGES),
                vmem(8, EDGES),
                vmem(8, EDGES),
                vmem(8, EDGES),
                vmem(8, EDGES),
                vmem(1, EDGES),
                vmem(9 * C, ATOMS),
                vmem(9 * C, ATOMS),
                vmem(9 * C, ATOMS),
                vmem(8 * C, EXT, dtype=BF16),
                vmem(4 * C, ATOMS),
                vmem(4 * C, BORDER),
                vmem(8, 4 * C, BORDER),
                vmem(8, 4 * C, BORDER),
                vmem(8, 4 * C, BORDER),
                vmem(8, BORDER),
                vmem(8, 8, BORDER),
                vmem(8, 8, BORDER),
                vmem(8, 8, BORDER),
                pltpu.SemaphoreType.DMA((4, 8)),
                pltpu.SemaphoreType.DMA((4, 8)),
            ],
            compiler_params=pltpu.CompilerParams(
                collective_id=0, has_side_effects=True, vmem_limit_bytes=63 * 2**20
            ),
        )(*args)

    def specs():
        lead = [P("dom", "sub", None, None), P("dom", "sub", None)]
        return (lead[0], lead[1], lead[1], lead[0]) + (P(),) * 13

    return jax.shard_map(
        body,
        mesh=mesh,
        in_specs=specs(),
        out_specs=(P("dom", "sub", None), P("dom", "sub", None, None)),
        check_vma=False,
    )
```

```python
import math

import jax
import jax.numpy as jnp
from jax import lax
from jax.experimental import pallas as pl
from jax.experimental.pallas import tpu as pltpu
from jax.sharding import PartitionSpec as P

CUTOFF = 5.0
MESH = pl.DeviceIdType.MESH
F32 = jnp.float32
BF16 = jnp.bfloat16
C = 128
SLOTS = 16
ATOMS = 256
BORDER = 128
EDGES = SLOTS * ATOMS
EXT = ATOMS + 8 * BORDER
SIDES = [(0, -1), (0, 1), (-1, 0), (1, 0), (-1, 1), (1, 1), (-1, -1), (1, -1)]
HALF = SLOTS ** (-0.5)


def dot(a, b):
    return jnp.dot(a, b, preferred_element_type=F32)


def dot_nt(a, b):
    return lax.dot_general(a, b, (((1,), (1,)), ((), ())), preferred_element_type=F32)


def split(x):
    high = x.astype(BF16)
    return high, (x - high.astype(F32)).astype(BF16)


def stack2(x):
    high = x.astype(BF16).astype(F32)
    return jnp.concatenate([high, x - high], axis=0).astype(BF16)


def stack4(x):
    high = x.astype(BF16).astype(F32)
    rest = x - high
    mid = rest.astype(BF16).astype(F32)
    return jnp.concatenate([high, mid, rest - mid, jnp.zeros_like(x)], axis=0).astype(BF16)


def turned(weight, copies=1):
    tall = weight.astype(F32)
    if copies > 1:
        tall = jnp.concatenate([tall] * copies, axis=0)
    return tall.T.astype(BF16)


def doubled(weight):
    return jnp.concatenate([weight, weight], axis=1)


def sine(z):
    z2 = z * z
    out = 1.0 / 6227020800.0
    for coefficient in (-1.0 / 39916800.0, 1.0 / 362880.0, -1.0 / 5040.0, 1.0 / 120.0, -1.0 / 6.0, 1.0):
        out = out * z2 + coefficient
    return out * z


def cosine(z):
    z2 = z * z
    out = 1.0 / 479001600.0 - z2 * (1.0 / 87178291200.0)
    for coefficient in (-1.0 / 3628800.0, 1.0 / 40320.0, -1.0 / 720.0, 1.0 / 24.0, -0.5, 1.0):
        out = out * z2 + coefficient
    return out


def sigmoid(x):
    return 1.0 / (1.0 + jnp.exp(-x))


def lanes(k, width=ATOMS):
    return pl.ds(pl.multiple_of(k * width, width), width)


def kernel(
    shape_of_mesh,
    inputs,
    energy_ref,
    force_ref,
    hot,
    listed,
    rad1,
    rad2,
    src1,
    src2,
    terms,
    slope1,
    slope2,
    basis,
    basis_slope,
    shift,
    harm,
    d_harm,
    d_radius,
    amps1,
    amps2,
    back,
    feats,
    out_feat,
    got_feat,
    out_grad,
    got_grad,
    out_pos,
    got_pos,
    out_force,
    got_force,
    send_sem,
    recv_sem,
    fetched,
    fetch_sem,
):
    n_dom, n_sub = shape_of_mesh
    dom = lax.axis_index("dom")
    sub = lax.axis_index("sub")

    toward = 1 - 2 * lax.rem(sub, 2)

    def device(a, b):
        return (lax.rem(dom + a + n_dom, n_dom), lax.rem(sub + b * toward + n_sub, n_sub))

    barrier = pltpu.get_barrier_semaphore()
    for a, b in SIDES:
        pl.semaphore_signal(barrier, inc=1, device_id=device(a, b), device_id_type=MESH)

    fetches = [
        pltpu.make_async_copy(source, target, fetch_sem.at[n])
        for n, (source, target) in enumerate(zip(inputs, fetched))
    ]
    for copy in fetches:
        copy.start()
    (
        pos_ref,
        spec_ref,
        bound_ref,
        neigh_ref,
        embed_ref,
        rad1_in_ref,
        rad1_out_ref,
        self1_ref,
        mix1_ref,
        gate1_ref,
        read1_ref,
        rad2_in_ref,
        rad2_out_ref,
        self2_ref,
        mix2_ref,
        out_in_ref,
        out_last_ref,
    ) = fetched

    def transfer(phase, source, target, o, side):
        return pltpu.make_async_remote_copy(
            src_ref=source,
            dst_ref=target,
            send_sem=send_sem.at[phase, o],
            recv_sem=recv_sem.at[phase, o],
            device_id=device(*side),
            device_id_type=MESH,
        )

    for copy in fetches[:4]:
        copy.wait()

    own_rows = jnp.concatenate(
        [pos_ref[:, 0, :], spec_ref[0].astype(F32), jnp.zeros((4, ATOMS), F32)], axis=0
    )
    border_hot = (
        lax.broadcasted_iota(jnp.int32, (ATOMS, BORDER), 0) == bound_ref[0]
    ).astype(F32).astype(BF16)
    picked = dot(stack4(own_rows), border_hot)
    out_pos[...] = picked[0:8] + picked[8:16] + picked[16:24]

    entries = neigh_ref[0, 0]
    number = lax.shift_right_logical(entries, 7)
    place = jnp.where(number < 2, number, EXT // BORDER)
    for o, (a, b) in enumerate(SIDES):
        place = jnp.where(number == 6 + 3 * a + b * toward, 2 + o, place)
    entries = place * BORDER + (entries & (BORDER - 1))
    for k in range(SLOTS):
        listed[:, k * ATOMS : (k + 1) * ATOMS] = entries[k : k + 1]

    def build(k, carry):
        at = lanes(k)
        ids = lax.broadcasted_iota(jnp.int32, (EXT, ATOMS), 0)
        hot[:, at] = jnp.where(ids == listed[:, at], 1.0, 0.0).astype(BF16)
        return carry

    lax.fori_loop(0, SLOTS // 2, build, 0)
    pl.semaphore_wait(barrier, 8)
    sent_pos = [transfer(0, out_pos, got_pos.at[o], o, (-a, b)) for o, (a, b) in enumerate(SIDES)]
    for copy in sent_pos:
        copy.start()
    lax.fori_loop(SLOTS // 2, SLOTS, build, 0)
    for copy in fetches[4:]:
        copy.wait()

    rad1_in_t = turned(rad1_in_ref[...], 2)
    rad1_out_t = turned(rad1_out_ref[...], 2)
    rad2_in_t = turned(rad2_in_ref[...], 2)
    rad2_out_t = turned(rad2_out_ref[...], 2)
    embed_t = turned(
        jnp.concatenate([embed_ref[...].astype(F32), jnp.zeros((6, C), F32)], axis=0)
    )

    for copy in sent_pos:
        copy.wait()
    table = stack4(jnp.concatenate([own_rows] + [got_pos[o] for o in range(8)], axis=1))

    def geometry(g, carry):
        at = lanes(g, 1024)
        found = dot(table, hot[:, at])
        there = found[0:8] + found[8:16] + found[16:24]
        here = jnp.concatenate([own_rows] * 4, axis=1)
        u = (there - here) * (1.0 / CUTOFF)
        shift[:, at] = u
        ux, uy, uz = u[0:1], u[1:2], u[2:3]
        r2 = ux * ux + uy * uy + uz * uz
        present = jnp.where(listed[:, at] < EXT, 1.0, 0.0)
        room = jnp.maximum(1.0 - r2, 0.0) * present
        orders = lax.broadcasted_iota(jnp.int32, (8, 1024), 0).astype(F32)
        turns = orders * jnp.minimum(r2, 1.0)
        turns = turns - 2.0 * jnp.floor(0.5 * turns + 0.5)
        z = (0.5 * math.pi) * turns
        sz, cz = sine(z), cosine(z)
        cos_n = 1.0 - 2.0 * sz * sz
        sin_n = 2.0 * sz * cz
        envelope = room * room
        base = envelope * cos_n
        basis[:, at] = base
        basis_slope[:, at] = -2.0 * room * cos_n - (math.pi * orders) * (envelope * sin_n)
        harm[0:1, at] = 1.7 * ux
        harm[1:2, at] = 1.7 * uy
        harm[2:3, at] = 1.7 * uz
        harm[3:4, at] = 3.9 * ux * uy
        harm[4:5, at] = 3.9 * uy * uz
        harm[5:6, at] = 1.1 * (3.0 * uz * uz - r2)
        harm[6:7, at] = 3.9 * ux * uz
        harm[7:8, at] = 1.95 * (ux * ux - uy * uy)
        kinds = lax.broadcasted_iota(jnp.int32, (16, 1024), 0).astype(F32)
        src1[:, at] = dot(embed_t, jnp.where(kinds == there[3:4], 1.0, 0.0).astype(BF16))
        radial(base, rad1_in_t, rad1_out_t, slope1, rad1, at)
        return carry

    def radial(base, in_t, out_t, slope, rad, at):
        pre = dot(in_t, stack2(base))
        gate = sigmoid(pre)
        slope[:, at] = gate * (1.0 + pre * (1.0 - gate))
        rad[:, at] = dot(out_t, stack2(pre * gate))

    lax.fori_loop(0, 4, geometry, 0)

    def aggregate(rad, src, amps, vectors):
        def step(t, carry):
            r = t * 8
            total = [jnp.zeros((8, ATOMS), F32) for _ in range(9)]
            for k in range(SLOTS):
                at = slice(k * ATOMS, (k + 1) * ATOMS)

                def rows(ref, block):
                    return ref[pl.ds(pl.multiple_of(block * C + r, 8), 8), at]

                s = rows(src, 0)
                total[0] += rows(rad, 0) * s
                p1 = rows(rad, 1) * s
                p2 = rows(rad, 2) * s
                for m in range(3):
                    total[1 + m] += p1 * harm[m : m + 1, at]
                for m in range(3, 8):
                    total[1 + m] += p2 * harm[m : m + 1, at]
                if vectors:
                    r3 = rows(rad, 3)
                    for m in range(3):
                        total[1 + m] += r3 * rows(src, 1 + m)
            for m in range(9):
                amps[pl.ds(pl.multiple_of(m * C + r, 8), 8), :] = total[m] * HALF
            return carry

        lax.fori_loop(0, C // 8, step, 0)

    def invariants(amps):
        a = [amps[m * C : (m + 1) * C, :] for m in range(9)]
        dipole = a[1] * a[1] + a[2] * a[2] + a[3] * a[3]
        quadrupole = a[4] * a[4] + a[5] * a[5] + a[6] * a[6] + a[7] * a[7] + a[8] * a[8]
        return jnp.concatenate([a[0], dipole, quadrupole], axis=0)

    aggregate(rad1, src1, amps1, False)
    own_kinds = lax.broadcasted_iota(jnp.int32, (16, ATOMS), 0)
    own_node = dot(embed_t, jnp.where(own_kinds == spec_ref[0], 1.0, 0.0).astype(BF16))
    scalars = dot(turned(self1_ref[...]), own_node.astype(BF16)) + dot(
        turned(mix1_ref[...], 2), stack2(invariants(amps1))
    )
    gating = sigmoid(dot(turned(gate1_ref[...], 2), stack2(scalars)))
    read = jnp.concatenate([jnp.broadcast_to(read1_ref[...], (C, C)).T] * 2, axis=1)
    energy_one = jnp.sum(read * scalars, axis=0, keepdims=True)
    own_feat = jnp.concatenate(
        [scalars] + [amps1[m * C : (m + 1) * C, :] * gating for m in range(1, 4)], axis=0
    )
    own_terms = stack2(own_feat)
    feats[:, 0:ATOMS] = own_terms
    picked_feat = dot(own_terms, border_hot)
    out_feat[...] = picked_feat[0:512] + picked_feat[512:1024]
    sent_feat = [
        transfer(1, out_feat, got_feat.at[0], 0, (0, -1)),
        transfer(1, out_feat, got_feat.at[1], 1, (0, 1)),
        transfer(1, out_feat, got_feat.at[2], 2, (1, 0)),
        transfer(1, out_feat, got_feat.at[3], 3, (-1, 0)),
        transfer(1, got_feat.at[2], got_feat.at[4], 4, (0, 1)),
        transfer(1, got_feat.at[3], got_feat.at[5], 5, (0, 1)),
        transfer(1, got_feat.at[0], got_feat.at[6], 6, (1, 0)),
        transfer(1, got_feat.at[0], got_feat.at[7], 7, (-1, 0)),
    ]
    for o in (0, 2, 3, 1):
        sent_feat[o].start()

    def second_radial(g, carry):
        at = lanes(g, 1024)
        radial(basis[:, at], rad2_in_t, rad2_out_t, slope2, rad2, at)
        return carry

    lax.fori_loop(0, 4, second_radial, 0)

    def gather(first, last):
        def step(g, carry):
            at = lanes(g, 1024)
            found = dot(feats[:, first:last], hot[first:last, at])
            found = found[0:512] + found[512:1024]
            src2[:, at] = found if first == 0 else src2[:, at] + found
            return carry

        lax.fori_loop(0, 4, step, 0)

    gather(0, ATOMS)
    for o, relayed in ((0, (6, 7)), (2, (4,)), (3, (5,))):
        sent_feat[o].wait_recv()
        for later in relayed:
            sent_feat[later].start()
    for pair in ((0, 1), (2, 3), (4, 5), (6, 7)):
        for o in pair:
            if o in (1, 4, 5, 6, 7):
                sent_feat[o].wait_recv()
            feats[:, ATOMS + o * BORDER : ATOMS + (o + 1) * BORDER] = stack2(got_feat[o])
        gather(ATOMS + pair[0] * BORDER, ATOMS + (pair[1] + 1) * BORDER)
    for copy in sent_feat:
        copy.wait_send()

    aggregate(rad2, src2, amps2, True)
    scalars_two = dot(turned(self2_ref[...], 2), stack2(scalars)) + dot(
        turned(mix2_ref[...], 2), stack2(invariants(amps2))
    )
    pre = dot(doubled(out_in_ref[...]), stack2(scalars_two))
    gate = sigmoid(pre)
    last = jnp.concatenate([jnp.broadcast_to(out_last_ref[...], (C, 16)).T] * 2, axis=1)
    energy_two = jnp.sum(last * (pre * gate), axis=0, keepdims=True)
    energy_ref[0] = energy_one + energy_two

    d_pre = last * (gate * (1.0 + pre * (1.0 - gate)))
    d_pre_high, d_pre_low = split(d_pre)
    out_in_wide = turned(out_in_ref[...])
    d_two = dot(out_in_wide, d_pre_high) + dot(out_in_wide, d_pre_low)
    d_two_terms = stack2(d_two)
    d_self = dot(doubled(self2_ref[...]), d_two_terms)
    d_inv = dot(doubled(mix2_ref[...]), d_two_terms)

    def to_back(amps, d_inv, extra):
        back[0:C, :] = d_inv[0:C] * HALF
        for m in range(1, 9):
            block = d_inv[C : 2 * C] if m < 4 else d_inv[2 * C : 3 * C]
            value = 2.0 * amps[m * C : (m + 1) * C, :] * block
            if extra is not None and m < 4:
                value = value + extra[m - 1]
            back[m * C : (m + 1) * C, :] = value * HALF

    to_back(amps2, d_inv, None)

    def source_grads(k, carry):
        at = lanes(k)
        for t in range(C // 16):
            b = [back[m * C + t * 16 : m * C + t * 16 + 16, :] for m in range(9)]
            r0, r1, r2, r3 = [rad2[l * C + t * 16 : l * C + t * 16 + 16, at] for l in range(4)]
            t1 = harm[0:1, at] * b[1] + harm[1:2, at] * b[2] + harm[2:3, at] * b[3]
            t2 = harm[3:4, at] * b[4]
            for m in range(4, 8):
                t2 = t2 + harm[m : m + 1, at] * b[m + 1]
            grads = [r0 * b[0] + r1 * t1 + r2 * t2] + [r3 * b[m] for m in range(1, 4)]
            for l in range(4):
                high, low = split(grads[l])
                terms[l * C + t * 16 : l * C + t * 16 + 16, at] = high
                terms[512 + l * C + t * 16 : 512 + l * C + t * 16 + 16, at] = low
        return carry

    lax.fori_loop(0, SLOTS, source_grads, 0)

    sent_grad = [
        transfer(2, out_grad.at[2], got_grad.at[0], 0, (0, -1)),
        transfer(2, out_grad.at[3], got_grad.at[1], 1, (0, 1)),
        transfer(2, out_grad.at[4], got_grad.at[2], 2, (-1, 0)),
        transfer(2, out_grad.at[5], got_grad.at[3], 3, (1, 0)),
        transfer(2, out_grad.at[6], got_grad.at[4], 4, (0, 1)),
        transfer(2, out_grad.at[7], got_grad.at[5], 5, (0, 1)),
        transfer(2, out_grad.at[8], got_grad.at[6], 6, (-1, 0)),
        transfer(2, out_grad.at[9], got_grad.at[7], 7, (1, 0)),
    ]

    def scatter(n, carry):
        tile = 4 - n
        summed = dot_nt(terms[...], hot[lanes(tile), :])
        summed = summed[0:512] + summed[512:1024]
        out_grad[2 * tile] = summed[:, 0:BORDER]
        out_grad[2 * tile + 1] = summed[:, BORDER : 2 * BORDER]

        @pl.when(n == 0)
        def _():
            sent_grad[6].start()
            sent_grad[7].start()

        @pl.when(n == 1)
        def _():
            sent_grad[4].start()
            sent_grad[5].start()

        @pl.when(n == 2)
        def _():
            for o in (2, 3):
                sent_grad[2 + o].wait_recv()
                out_grad[2 + o] = out_grad[2 + o] + got_grad[2 + o]
                sent_grad[o].start()

        @pl.when(n == 3)
        def _():
            sent_grad[1].start()
            sent_grad[6].wait_recv()
            sent_grad[7].wait_recv()
            out_grad[2] = out_grad[2] + got_grad[6] + got_grad[7]
            sent_grad[0].start()

        return carry

    lax.fori_loop(0, 5, scatter, 0)

    def radial_grads(rad, src, slope, in_ref, out_ref, blocks, first):
        out_pair = doubled(out_ref[...])

        def step(k, carry):
            at = lanes(k)
            total = [jnp.zeros((8, ATOMS), F32) for _ in range(8)]
            for t in range(C // 16):
                b = [back[m * C + t * 16 : m * C + t * 16 + 16, :] for m in range(9)]
                t1 = harm[0:1, at] * b[1] + harm[1:2, at] * b[2] + harm[2:3, at] * b[3]
                t2 = harm[3:4, at] * b[4]
                for m in range(4, 8):
                    t2 = t2 + harm[m : m + 1, at] * b[m + 1]
                s = src[t * 16 : t * 16 + 16, at]
                grads = [s * b[0], s * t1, s * t2]
                if blocks == 4:
                    v = [src[l * C + t * 16 : l * C + t * 16 + 16, at] for l in range(1, 4)]
                    grads.append(v[0] * b[1] + v[1] * b[2] + v[2] * b[3])
                for l in range(blocks):
                    high, low = split(grads[l])
                    terms[l * C + t * 16 : l * C + t * 16 + 16, at] = high
                    terms[
                        (blocks + l) * C + t * 16 : (blocks + l) * C + t * 16 + 16, at
                    ] = low
                p1 = rad[C + t * 16 : C + t * 16 + 16, at] * s
                p2 = rad[2 * C + t * 16 : 2 * C + t * 16 + 16, at] * s
                for m in range(8):
                    product = (p1 if m < 3 else p2) * b[m + 1]
                    total[m] += product[0:8] + product[8:16]
            for m in range(8):
                value = jnp.sum(total[m], axis=0, keepdims=True)
                if not first:
                    value = value + d_harm[m : m + 1, at]
                d_harm[m : m + 1, at] = value
            return carry

        lax.fori_loop(0, SLOTS, step, 0)

        def tail(g, carry):
            at = lanes(g, 1024)
            d_hidden = dot(out_pair, terms[0 : 2 * blocks * C, at]) * slope[:, at]
            high, low = split(d_hidden)
            d_basis = dot(in_ref[...], high) + dot(in_ref[...], low)
            value = jnp.sum(d_basis * basis_slope[:, at], axis=0, keepdims=True)
            if not first:
                value = value + d_radius[:, at]
            d_radius[:, at] = value
            return carry

        lax.fori_loop(0, 4, tail, 0)

    radial_grads(rad2, src2, slope2, rad2_in_ref, rad2_out_ref, 4, True)

    for copy in sent_grad[:4]:
        copy.wait_recv()
    for copy in sent_grad:
        copy.wait_send()
    returned = got_grad[0]
    for o in range(1, 4):
        returned = returned + got_grad[o]
    placed = dot_nt(stack2(returned), border_hot)
    d_feat = jnp.concatenate([out_grad[0], out_grad[1]], axis=1) + placed[0:512] + placed[512:1024]
    d_vec = [d_feat[m * C : (m + 1) * C] for m in range(1, 4)]
    d_gate = (
        d_vec[0] * amps1[C : 2 * C, :]
        + d_vec[1] * amps1[2 * C : 3 * C, :]
        + d_vec[2] * amps1[3 * C : 4 * C, :]
    ) * (gating * (1.0 - gating))
    d_scalars = d_feat[0:C] + d_self + read + dot(doubled(gate1_ref[...]), stack2(d_gate))
    d_inv_one = dot(doubled(mix1_ref[...]), stack2(d_scalars))
    to_back(amps1, d_inv_one, [d * gating for d in d_vec])
    radial_grads(rad1, src1, slope1, rad1_in_ref, rad1_out_ref, 3, False)

    def to_shift(g, carry):
        at = lanes(g, 1024)
        ux, uy, uz = [shift[m : m + 1, at] for m in range(3)]
        d = [d_harm[m : m + 1, at] for m in range(8)]
        dr = 2.0 * (d_radius[:, at] - 1.1 * d[5])
        basis[0:1, at] = (
            1.7 * d[0] + 3.9 * (uy * d[3] + uz * d[6] + ux * d[7]) + ux * dr
        ) * (1.0 / CUTOFF)
        basis[1:2, at] = (
            1.7 * d[1] + 3.9 * (ux * d[3] + uz * d[4] - uy * d[7]) + uy * dr
        ) * (1.0 / CUTOFF)
        basis[2:3, at] = (
            1.7 * d[2] + 3.9 * (uy * d[4] + ux * d[6]) + uz * (6.6 * d[5] + dr)
        ) * (1.0 / CUTOFF)
        basis[3:8, at] = jnp.zeros((5, 1024), F32)
        return carry

    lax.fori_loop(0, 4, to_shift, 0)
    d_edges = stack4(basis[...])
    sent_force = [
        transfer(3, out_force.at[o], got_force.at[o], o, side) for o, side in enumerate(SIDES)
    ]
    for n in (4, 3, 2, 1, 0):
        summed = dot_nt(d_edges, hot[n * 256 : (n + 1) * 256, :])
        summed = summed[0:8] + summed[8:16] + summed[16:24]
        if n > 0:
            for o in (2 * n - 2, 2 * n - 1):
                out_force[o] = summed[:, (o % 2) * BORDER : (o % 2 + 1) * BORDER]
                sent_force[o].start()
    own_force = summed
    for k in range(SLOTS):
        own_force = own_force - basis[:, k * ATOMS : (k + 1) * ATOMS]
    for copy in sent_force:
        copy.wait()
    returned = got_force[0]
    for o in range(1, 8):
        returned = returned + got_force[o]
    placed = dot_nt(stack4(returned), border_hot)
    own_force = own_force + placed[0:8] + placed[8:16] + placed[16:24]
    for m in range(3):
        force_ref[m] = -own_force[m : m + 1]


def solution(mesh):
    shape_of_mesh = (mesh.shape["dom"], mesh.shape["sub"])

    def vmem(*shape, dtype=F32):
        return pltpu.VMEM(shape, dtype)

    def body(*args):
        args = list(args)
        args[0] = args[0].reshape(3, 1, ATOMS)
        args[10] = args[10].reshape(1, C)
        args[15] = args[15].T
        args[16] = args[16].reshape(1, 16)

        def run(*refs):
            kernel(shape_of_mesh, refs[:17], *refs[17:-2], refs[-2], refs[-1])

        energies, forces = pl.pallas_call(
            run,
            out_shape=(
                jax.ShapeDtypeStruct((1, 1, ATOMS), F32),
                jax.ShapeDtypeStruct((3, 1, ATOMS), F32),
            ),
            in_specs=[pl.BlockSpec(memory_space=pl.ANY)] * 17,
            out_specs=[pl.BlockSpec(memory_space=pltpu.VMEM)] * 2,
            scratch_shapes=[
                vmem(EXT, EDGES, dtype=BF16),
                vmem(1, EDGES, dtype=jnp.int32),
                vmem(3 * C, EDGES),
                vmem(4 * C, EDGES),
                vmem(C, EDGES),
                vmem(4 * C, EDGES),
                vmem(8 * C, EDGES, dtype=BF16),
                vmem(64, EDGES),
                vmem(64, EDGES),
                vmem(8, EDGES),
                vmem(8, EDGES),
                vmem(8, EDGES),
                vmem(8, EDGES),
                vmem(8, EDGES),
                vmem(1, EDGES),
                vmem(9 * C, ATOMS),
                vmem(9 * C, ATOMS),
                vmem(9 * C, ATOMS),
                vmem(8 * C, EXT, dtype=BF16),
                vmem(4 * C, BORDER),
                vmem(8, 4 * C, BORDER),
                vmem(10, 4 * C, BORDER),
                vmem(8, 4 * C, BORDER),
                vmem(8, BORDER),
                vmem(8, 8, BORDER),
                vmem(8, 8, BORDER),
                vmem(8, 8, BORDER),
                pltpu.SemaphoreType.DMA((4, 8)),
                pltpu.SemaphoreType.DMA((4, 8)),
                [vmem(*arg.shape, dtype=arg.dtype) for arg in args],
                pltpu.SemaphoreType.DMA((17,)),
            ],
            compiler_params=pltpu.CompilerParams(
                collective_id=0, has_side_effects=True, vmem_limit_bytes=63 * 2**20
            ),
        )(*args)
        return energies, forces.reshape(1, 1, 3, ATOMS)

    def specs():
        lead = [P("dom", "sub", None, None), P("dom", "sub", None)]
        return (lead[0], lead[1], lead[1], lead[0]) + (P(),) * 13

    return jax.shard_map(
        body,
        mesh=mesh,
        in_specs=specs(),
        out_specs=(P("dom", "sub", None), P("dom", "sub", None, None)),
        check_vma=False,
    )
```

```python
import math

import jax
import jax.numpy as jnp
from jax import lax
from jax.experimental import pallas as pl
from jax.experimental.pallas import tpu as pltpu
from jax.sharding import PartitionSpec as P

CUTOFF = 5.0
MESH = pl.DeviceIdType.MESH
F32 = jnp.float32
BF16 = jnp.bfloat16
C = 128
SLOTS = 16
ATOMS = 256
BORDER = 128
EDGES = SLOTS * ATOMS
EXT = ATOMS + 8 * BORDER
SIDES = [(0, -1), (0, 1), (-1, 0), (1, 0), (-1, 1), (1, 1), (-1, -1), (1, -1)]
HALF = SLOTS ** (-0.5)


def dot(a, b):
    return jnp.dot(a, b, preferred_element_type=F32)


def dot_nt(a, b):
    return lax.dot_general(a, b, (((1,), (1,)), ((), ())), preferred_element_type=F32)


def split(x):
    high = x.astype(BF16)
    return high, (x - high.astype(F32)).astype(BF16)


def stack2(x):
    high = x.astype(BF16).astype(F32)
    return jnp.concatenate([high, x - high], axis=0).astype(BF16)


def stack4(x):
    high = x.astype(BF16).astype(F32)
    rest = x - high
    mid = rest.astype(BF16).astype(F32)
    return jnp.concatenate([high, mid, rest - mid, jnp.zeros_like(x)], axis=0).astype(BF16)


def turned(weight, copies=1):
    tall = weight.astype(F32)
    if copies > 1:
        tall = jnp.concatenate([tall] * copies, axis=0)
    return tall.T.astype(BF16)


def doubled(weight):
    return jnp.concatenate([weight, weight], axis=1)


def sine(z):
    z2 = z * z
    out = 1.0 / 6227020800.0
    for coefficient in (-1.0 / 39916800.0, 1.0 / 362880.0, -1.0 / 5040.0, 1.0 / 120.0, -1.0 / 6.0, 1.0):
        out = out * z2 + coefficient
    return out * z


def cosine(z):
    z2 = z * z
    out = 1.0 / 479001600.0 - z2 * (1.0 / 87178291200.0)
    for coefficient in (-1.0 / 3628800.0, 1.0 / 40320.0, -1.0 / 720.0, 1.0 / 24.0, -0.5, 1.0):
        out = out * z2 + coefficient
    return out


def sigmoid(x):
    return 1.0 / (1.0 + jnp.exp(-x))


def lanes(k, width=ATOMS):
    return pl.ds(pl.multiple_of(k * width, width), width)


def kernel(
    shape_of_mesh,
    inputs,
    energy_ref,
    force_ref,
    hot,
    listed,
    rad1,
    rad2,
    src1,
    src2,
    terms,
    slope1,
    slope2,
    basis,
    basis_slope,
    shift,
    harm,
    d_harm,
    d_radius,
    amps1,
    amps2,
    back,
    feats,
    out_feat,
    got_feat,
    out_grad,
    got_grad,
    out_pos,
    got_pos,
    out_force,
    got_force,
    send_sem,
    recv_sem,
    fetched,
    fetch_sem,
):
    n_dom, n_sub = shape_of_mesh
    dom = lax.axis_index("dom")
    sub = lax.axis_index("sub")

    toward = 1 - 2 * lax.rem(sub, 2)

    def device(a, b):
        return (lax.rem(dom + a + n_dom, n_dom), lax.rem(sub + b * toward + n_sub, n_sub))

    barrier = pltpu.get_barrier_semaphore()
    for a, b in SIDES:
        pl.semaphore_signal(barrier, inc=1, device_id=device(a, b), device_id_type=MESH)

    fetches = [
        pltpu.make_async_copy(source, target, fetch_sem.at[n])
        for n, (source, target) in enumerate(zip(inputs, fetched))
    ]
    for copy in fetches:
        copy.start()
    (
        pos_ref,
        spec_ref,
        bound_ref,
        neigh_ref,
        embed_ref,
        rad1_in_ref,
        rad1_out_ref,
        self1_ref,
        mix1_ref,
        gate1_ref,
        read1_ref,
        rad2_in_ref,
        rad2_out_ref,
        self2_ref,
        mix2_ref,
        out_in_ref,
        out_last_ref,
    ) = fetched

    def transfer(phase, source, target, o, side):
        return pltpu.make_async_remote_copy(
            src_ref=source,
            dst_ref=target,
            send_sem=send_sem.at[phase, o],
            recv_sem=recv_sem.at[phase, o],
            device_id=device(*side),
            device_id_type=MESH,
        )

    for copy in fetches[:4]:
        copy.wait()

    own_rows = jnp.concatenate(
        [pos_ref[:, 0, :], spec_ref[0].astype(F32), jnp.zeros((4, ATOMS), F32)], axis=0
    )
    border_hot = (
        lax.broadcasted_iota(jnp.int32, (ATOMS, BORDER), 0) == bound_ref[0]
    ).astype(F32).astype(BF16)
    picked = dot(stack4(own_rows), border_hot)
    out_pos[...] = picked[0:8] + picked[8:16] + picked[16:24]

    entries = neigh_ref[0, 0]
    number = lax.shift_right_logical(entries, 7)
    place = jnp.where(number < 2, number, EXT // BORDER)
    for o, (a, b) in enumerate(SIDES):
        place = jnp.where(number == 6 + 3 * a + b * toward, 2 + o, place)
    entries = place * BORDER + (entries & (BORDER - 1))
    for k in range(SLOTS):
        listed[:, k * ATOMS : (k + 1) * ATOMS] = entries[k : k + 1]

    def build(k, carry):
        at = lanes(k)
        ids = lax.broadcasted_iota(jnp.int32, (EXT, ATOMS), 0)
        hot[:, at] = jnp.where(ids == listed[:, at], 1.0, 0.0).astype(BF16)
        return carry

    lax.fori_loop(0, SLOTS // 2, build, 0)
    pl.semaphore_wait(barrier, 8)
    sent_pos = [transfer(0, out_pos, got_pos.at[o], o, (-a, b)) for o, (a, b) in enumerate(SIDES)]
    for copy in sent_pos:
        copy.start()
    lax.fori_loop(SLOTS // 2, SLOTS, build, 0)
    for copy in fetches[4:]:
        copy.wait()

    self1_t = turned(self1_ref[...])
    mix1_t = turned(mix1_ref[...], 2)
    gate1_t = turned(gate1_ref[...], 2)
    self2_t = turned(self2_ref[...], 2)
    mix2_t = turned(mix2_ref[...], 2)
    out_in_wide = turned(out_in_ref[...])
    read = jnp.concatenate([jnp.broadcast_to(read1_ref[...], (C, C)).T] * 2, axis=1)
    last = jnp.concatenate([jnp.broadcast_to(out_last_ref[...], (C, 16)).T] * 2, axis=1)
    rad1_in_t = turned(rad1_in_ref[...], 2)
    rad1_out_t = turned(rad1_out_ref[...], 2)
    rad2_in_t = turned(rad2_in_ref[...], 2)
    rad2_out_t = turned(rad2_out_ref[...], 2)
    embed_t = turned(
        jnp.concatenate([embed_ref[...].astype(F32), jnp.zeros((6, C), F32)], axis=0)
    )

    for copy in sent_pos:
        copy.wait()
    blocks = [own_rows[0:4, 0:BORDER], own_rows[0:4, BORDER:]] + [got_pos[o][0:4] for o in range(8)]
    table = [jnp.concatenate(blocks[n : n + 2], axis=0) for n in range(0, 10, 2)]

    def geometry(g, carry):
        at = lanes(g, 1024)
        there = []
        for part in range(8):
            ids = listed[:, pl.ds(pl.multiple_of(g * 1024 + part * 128, 128), 128)]
            ids = jnp.broadcast_to(ids, (8, 128))
            inside = ids & (BORDER - 1)
            block = lax.shift_right_logical(ids, 7)
            found = jnp.zeros((8, 128), F32)
            for n in range(5):
                taken = jnp.take_along_axis(table[n], inside, axis=1, mode="promise_in_bounds")
                found = jnp.where(lax.shift_right_logical(block, 1) == n, taken, found)
            there.append(jnp.where((block & 1)[0:4] == 1, found[4:8], found[0:4]))
        there = jnp.concatenate(there, axis=1)
        here = jnp.concatenate([own_rows[0:4]] * 4, axis=1)
        u = (there - here) * (1.0 / CUTOFF)
        shift[0:4, at] = u
        ux, uy, uz = u[0:1], u[1:2], u[2:3]
        r2 = ux * ux + uy * uy + uz * uz
        present = jnp.where(listed[:, at] < EXT, 1.0, 0.0)
        room = jnp.maximum(1.0 - r2, 0.0) * present
        orders = lax.broadcasted_iota(jnp.int32, (8, 1024), 0).astype(F32)
        turns = orders * jnp.minimum(r2, 1.0)
        turns = turns - 2.0 * jnp.floor(0.5 * turns + 0.5)
        z = (0.5 * math.pi) * turns
        sz, cz = sine(z), cosine(z)
        cos_n = 1.0 - 2.0 * sz * sz
        sin_n = 2.0 * sz * cz
        envelope = room * room
        base = envelope * cos_n
        basis[:, at] = base
        basis_slope[:, at] = -2.0 * room * cos_n - (math.pi * orders) * (envelope * sin_n)
        harm[0:1, at] = 1.7 * ux
        harm[1:2, at] = 1.7 * uy
        harm[2:3, at] = 1.7 * uz
        harm[3:4, at] = 3.9 * ux * uy
        harm[4:5, at] = 3.9 * uy * uz
        harm[5:6, at] = 1.1 * (3.0 * uz * uz - r2)
        harm[6:7, at] = 3.9 * ux * uz
        harm[7:8, at] = 1.95 * (ux * ux - uy * uy)
        kinds = lax.broadcasted_iota(jnp.int32, (16, 1024), 0).astype(F32)
        src1[:, at] = dot(embed_t, jnp.where(kinds == there[3:4], 1.0, 0.0).astype(BF16))
        radial(base, rad1_in_t, rad1_out_t, slope1, rad1, at)
        return carry

    def radial(base, in_t, out_t, slope, rad, at):
        pre = dot(in_t, stack2(base))
        gate = sigmoid(pre)
        slope[:, at] = gate * (1.0 + pre * (1.0 - gate))
        rad[:, at] = dot(out_t, stack2(pre * gate))

    lax.fori_loop(0, 4, geometry, 0)

    def aggregate(rad, src, amps, vectors):
        def step(t, carry):
            r = t * 8
            total = [jnp.zeros((8, ATOMS), F32) for _ in range(9)]
            for k in range(SLOTS):
                at = slice(k * ATOMS, (k + 1) * ATOMS)

                def rows(ref, block):
                    return ref[pl.ds(pl.multiple_of(block * C + r, 8), 8), at]

                s = rows(src, 0)
                total[0] += rows(rad, 0) * s
                p1 = rows(rad, 1) * s
                p2 = rows(rad, 2) * s
                for m in range(3):
                    total[1 + m] += p1 * harm[m : m + 1, at]
                for m in range(3, 8):
                    total[1 + m] += p2 * harm[m : m + 1, at]
                if vectors:
                    r3 = rows(rad, 3)
                    for m in range(3):
                        total[1 + m] += r3 * rows(src, 1 + m)
            for m in range(9):
                amps[pl.ds(pl.multiple_of(m * C + r, 8), 8), :] = total[m] * HALF
            return carry

        lax.fori_loop(0, C // 8, step, 0)

    def invariants(amps):
        a = [amps[m * C : (m + 1) * C, :] for m in range(9)]
        dipole = a[1] * a[1] + a[2] * a[2] + a[3] * a[3]
        quadrupole = a[4] * a[4] + a[5] * a[5] + a[6] * a[6] + a[7] * a[7] + a[8] * a[8]
        return jnp.concatenate([a[0], dipole, quadrupole], axis=0)

    aggregate(rad1, src1, amps1, False)
    own_kinds = lax.broadcasted_iota(jnp.int32, (16, ATOMS), 0)
    own_node = dot(embed_t, jnp.where(own_kinds == spec_ref[0], 1.0, 0.0).astype(BF16))
    scalars = dot(self1_t, own_node.astype(BF16)) + dot(
        mix1_t, stack2(invariants(amps1))
    )
    gating = sigmoid(dot(gate1_t, stack2(scalars)))
    energy_one = jnp.sum(read * scalars, axis=0, keepdims=True)
    own_feat = jnp.concatenate(
        [scalars] + [amps1[m * C : (m + 1) * C, :] * gating for m in range(1, 4)], axis=0
    )
    for half in range(2):
        feats[half * 512 : half * 512 + 512, 0:ATOMS] = stack2(
            own_feat[half * 256 : half * 256 + 256]
        )
    picked_feat = dot(feats[:, 0:ATOMS], border_hot)
    for half in range(2):
        at = half * 512
        out_feat[half * 256 : half * 256 + 256] = (
            picked_feat[at : at + 256] + picked_feat[at + 256 : at + 512]
        )
    def feature_way(half, source, o, side):
        rows = pl.ds(half * 256, 256)
        return transfer(1 + 3 * half, source.at[rows], got_feat.at[o, rows], o, side)

    sent_feat = [
        [
            feature_way(half, out_feat, 0, (0, -1)),
            feature_way(half, out_feat, 1, (0, 1)),
            feature_way(half, out_feat, 2, (1, 0)),
            feature_way(half, out_feat, 3, (-1, 0)),
            feature_way(half, got_feat.at[2], 4, (0, 1)),
            feature_way(half, got_feat.at[3], 5, (0, 1)),
            feature_way(half, got_feat.at[0], 6, (1, 0)),
            feature_way(half, got_feat.at[0], 7, (-1, 0)),
        ]
        for half in range(2)
    ]
    for half in range(2):
        for o in (0, 2, 3, 1):
            sent_feat[half][o].start()

    def second_radial(g, carry):
        at = lanes(g, 1024)
        radial(basis[:, at], rad2_in_t, rad2_out_t, slope2, rad2, at)
        return carry

    lax.fori_loop(0, 4, second_radial, 0)

    self_part = dot(self2_t, stack2(scalars))

    def gather(tile, halves):
        def step(g, carry):
            at = lanes(g, 1024)
            rows = slice(halves[0] * 512, halves[-1] * 512 + 512)
            cols = slice(tile * 256, tile * 256 + 256)
            found = dot(feats[rows, cols], hot[cols, at])
            for n, half in enumerate(halves):
                to = slice(half * 256, half * 256 + 256)
                value = found[n * 512 : n * 512 + 256] + found[n * 512 + 256 : n * 512 + 512]
                src2[to, at] = value if tile == 0 else src2[to, at] + value
            return carry

        lax.fori_loop(0, 4, step, 0)

    def arrived(tile, half):
        for o in (2 * tile - 2, 2 * tile - 1):
            feats[half * 512 : half * 512 + 512, ATOMS + o * BORDER : ATOMS + (o + 1) * BORDER] = (
                stack2(got_feat[o, half * 256 : half * 256 + 256])
            )

    gather(0, (0, 1))
    for half in range(2):
        for o, relayed in ((0, (6, 7)), (2, (4,)), (3, (5,))):
            sent_feat[half][o].wait_recv()
            for later in relayed:
                sent_feat[half][later].start()
        sent_feat[half][1].wait_recv()
        for tile in (1, 2):
            arrived(tile, half)
            gather(tile, (half,))
    for tile in (3, 4):
        for half in range(2):
            for o in (2 * tile - 2, 2 * tile - 1):
                sent_feat[half][o].wait_recv()
            arrived(tile, half)
        gather(tile, (0, 1))
    for half in range(2):
        for copy in sent_feat[half]:
            copy.wait_send()
    aggregate(rad2, src2, amps2, True)
    scalars_two = self_part + dot(mix2_t, stack2(invariants(amps2)))
    pre = dot(doubled(out_in_ref[...]), stack2(scalars_two))
    gate = sigmoid(pre)
    energy_two = jnp.sum(last * (pre * gate), axis=0, keepdims=True)
    energy_ref[0] = energy_one + energy_two

    d_pre = last * (gate * (1.0 + pre * (1.0 - gate)))
    d_pre_high, d_pre_low = split(d_pre)
    d_two = dot(out_in_wide, d_pre_high) + dot(out_in_wide, d_pre_low)
    d_two_terms = stack2(d_two)
    d_self = dot(doubled(self2_ref[...]), d_two_terms)
    d_inv = dot(doubled(mix2_ref[...]), d_two_terms)

    def to_back(amps, d_inv, extra):
        back[0:C, :] = d_inv[0:C] * HALF
        for m in range(1, 9):
            block = d_inv[C : 2 * C] if m < 4 else d_inv[2 * C : 3 * C]
            value = 2.0 * amps[m * C : (m + 1) * C, :] * block
            if extra is not None and m < 4:
                value = value + extra[m - 1]
            back[m * C : (m + 1) * C, :] = value * HALF

    to_back(amps2, d_inv, None)

    def source_grads(k, carry):
        at = lanes(k)
        for t in range(C // 16):
            b = [back[m * C + t * 16 : m * C + t * 16 + 16, :] for m in range(9)]
            r0, r1, r2, r3 = [rad2[l * C + t * 16 : l * C + t * 16 + 16, at] for l in range(4)]
            t1 = harm[0:1, at] * b[1] + harm[1:2, at] * b[2] + harm[2:3, at] * b[3]
            t2 = harm[3:4, at] * b[4]
            for m in range(4, 8):
                t2 = t2 + harm[m : m + 1, at] * b[m + 1]
            grads = [r0 * b[0] + r1 * t1 + r2 * t2] + [r3 * b[m] for m in range(1, 4)]
            for l in range(4):
                high, low = split(grads[l])
                terms[l * C + t * 16 : l * C + t * 16 + 16, at] = high
                terms[512 + l * C + t * 16 : 512 + l * C + t * 16 + 16, at] = low
        return carry

    lax.fori_loop(0, SLOTS, source_grads, 0)

    sent_grad = [
        transfer(2, out_grad.at[2], got_grad.at[0], 0, (0, -1)),
        transfer(2, out_grad.at[3], got_grad.at[1], 1, (0, 1)),
        transfer(2, out_grad.at[4], got_grad.at[2], 2, (-1, 0)),
        transfer(2, out_grad.at[5], got_grad.at[3], 3, (1, 0)),
        transfer(2, out_grad.at[6], got_grad.at[4], 4, (0, 1)),
        transfer(2, out_grad.at[7], got_grad.at[5], 5, (0, 1)),
        transfer(2, out_grad.at[8], got_grad.at[6], 6, (-1, 0)),
        transfer(2, out_grad.at[9], got_grad.at[7], 7, (1, 0)),
    ]

    def scatter(n, carry):
        tile = 4 - n
        summed = dot_nt(terms[...], hot[lanes(tile), :])
        summed = summed[0:512] + summed[512:1024]
        out_grad[2 * tile] = summed[:, 0:BORDER]
        out_grad[2 * tile + 1] = summed[:, BORDER : 2 * BORDER]

        @pl.when(n == 0)
        def _():
            sent_grad[6].start()
            sent_grad[7].start()

        @pl.when(n == 1)
        def _():
            sent_grad[4].start()
            sent_grad[5].start()

        @pl.when(n == 2)
        def _():
            for o in (2, 3):
                sent_grad[2 + o].wait_recv()
                out_grad[2 + o] = out_grad[2 + o] + got_grad[2 + o]
                sent_grad[o].start()

        @pl.when(n == 3)
        def _():
            sent_grad[1].start()
            sent_grad[6].wait_recv()
            sent_grad[7].wait_recv()
            out_grad[2] = out_grad[2] + got_grad[6] + got_grad[7]
            sent_grad[0].start()

        return carry

    lax.fori_loop(0, 5, scatter, 0)

    def radial_grads(rad, src, slope, in_ref, out_ref, blocks, first):
        out_pair = doubled(out_ref[...])

        def step(k, carry):
            at = lanes(k)
            total = [jnp.zeros((8, ATOMS), F32) for _ in range(8)]
            for t in range(C // 16):
                b = [back[m * C + t * 16 : m * C + t * 16 + 16, :] for m in range(9)]
                t1 = harm[0:1, at] * b[1] + harm[1:2, at] * b[2] + harm[2:3, at] * b[3]
                t2 = harm[3:4, at] * b[4]
                for m in range(4, 8):
                    t2 = t2 + harm[m : m + 1, at] * b[m + 1]
                s = src[t * 16 : t * 16 + 16, at]
                grads = [s * b[0], s * t1, s * t2]
                if blocks == 4:
                    v = [src[l * C + t * 16 : l * C + t * 16 + 16, at] for l in range(1, 4)]
                    grads.append(v[0] * b[1] + v[1] * b[2] + v[2] * b[3])
                for l in range(blocks):
                    high, low = split(grads[l])
                    terms[l * C + t * 16 : l * C + t * 16 + 16, at] = high
                    terms[
                        (blocks + l) * C + t * 16 : (blocks + l) * C + t * 16 + 16, at
                    ] = low
                p1 = rad[C + t * 16 : C + t * 16 + 16, at] * s
                p2 = rad[2 * C + t * 16 : 2 * C + t * 16 + 16, at] * s
                for m in range(8):
                    product = (p1 if m < 3 else p2) * b[m + 1]
                    total[m] += product[0:8] + product[8:16]
            for m in range(8):
                value = jnp.sum(total[m], axis=0, keepdims=True)
                if not first:
                    value = value + d_harm[m : m + 1, at]
                d_harm[m : m + 1, at] = value
            return carry

        lax.fori_loop(0, SLOTS, step, 0)

        def tail(g, carry):
            at = lanes(g, 1024)
            d_hidden = dot(out_pair, terms[0 : 2 * blocks * C, at]) * slope[:, at]
            high, low = split(d_hidden)
            d_basis = dot(in_ref[...], high) + dot(in_ref[...], low)
            value = jnp.sum(d_basis * basis_slope[:, at], axis=0, keepdims=True)
            if not first:
                value = value + d_radius[:, at]
            d_radius[:, at] = value
            return carry

        lax.fori_loop(0, 4, tail, 0)

    radial_grads(rad2, src2, slope2, rad2_in_ref, rad2_out_ref, 4, True)

    for copy in sent_grad[:4]:
        copy.wait_recv()
    for copy in sent_grad:
        copy.wait_send()
    returned = got_grad[0]
    for o in range(1, 4):
        returned = returned + got_grad[o]
    placed = dot_nt(stack2(returned), border_hot)
    d_feat = jnp.concatenate([out_grad[0], out_grad[1]], axis=1) + placed[0:512] + placed[512:1024]
    d_vec = [d_feat[m * C : (m + 1) * C] for m in range(1, 4)]
    d_gate = (
        d_vec[0] * amps1[C : 2 * C, :]
        + d_vec[1] * amps1[2 * C : 3 * C, :]
        + d_vec[2] * amps1[3 * C : 4 * C, :]
    ) * (gating * (1.0 - gating))
    d_scalars = d_feat[0:C] + d_self + read + dot(doubled(gate1_ref[...]), stack2(d_gate))
    d_inv_one = dot(doubled(mix1_ref[...]), stack2(d_scalars))
    to_back(amps1, d_inv_one, [d * gating for d in d_vec])
    radial_grads(rad1, src1, slope1, rad1_in_ref, rad1_out_ref, 3, False)

    def to_shift(g, carry):
        at = lanes(g, 1024)
        ux, uy, uz = [shift[m : m + 1, at] for m in range(3)]
        d = [d_harm[m : m + 1, at] for m in range(8)]
        dr = 2.0 * (d_radius[:, at] - 1.1 * d[5])
        basis[0:1, at] = (
            1.7 * d[0] + 3.9 * (uy * d[3] + uz * d[6] + ux * d[7]) + ux * dr
        ) * (1.0 / CUTOFF)
        basis[1:2, at] = (
            1.7 * d[1] + 3.9 * (ux * d[3] + uz * d[4] - uy * d[7]) + uy * dr
        ) * (1.0 / CUTOFF)
        basis[2:3, at] = (
            1.7 * d[2] + 3.9 * (uy * d[4] + ux * d[6]) + uz * (6.6 * d[5] + dr)
        ) * (1.0 / CUTOFF)
        basis[3:8, at] = jnp.zeros((5, 1024), F32)
        return carry

    lax.fori_loop(0, 4, to_shift, 0)
    d_edges = stack4(basis[...])
    sent_force = [
        transfer(3, out_force.at[o], got_force.at[o], o, side) for o, side in enumerate(SIDES)
    ]
    for n in (4, 3, 2, 1, 0):
        summed = dot_nt(d_edges, hot[n * 256 : (n + 1) * 256, :])
        summed = summed[0:8] + summed[8:16] + summed[16:24]
        if n > 0:
            for o in (2 * n - 2, 2 * n - 1):
                out_force[o] = summed[:, (o % 2) * BORDER : (o % 2 + 1) * BORDER]
                sent_force[o].start()
    own_force = summed
    for k in range(SLOTS):
        own_force = own_force - basis[:, k * ATOMS : (k + 1) * ATOMS]
    for copy in sent_force:
        copy.wait()
    returned = got_force[0]
    for o in range(1, 8):
        returned = returned + got_force[o]
    placed = dot_nt(stack4(returned), border_hot)
    own_force = own_force + placed[0:8] + placed[8:16] + placed[16:24]
    for m in range(3):
        force_ref[m] = -own_force[m : m + 1]


def solution(mesh):
    shape_of_mesh = (mesh.shape["dom"], mesh.shape["sub"])

    def vmem(*shape, dtype=F32):
        return pltpu.VMEM(shape, dtype)

    def body(*args):
        args = list(args)
        args[0] = args[0].reshape(3, 1, ATOMS)
        args[10] = args[10].reshape(1, C)
        args[15] = args[15].T
        args[16] = args[16].reshape(1, 16)

        def run(*refs):
            kernel(shape_of_mesh, refs[:17], *refs[17:-2], refs[-2], refs[-1])

        energies, forces = pl.pallas_call(
            run,
            out_shape=(
                jax.ShapeDtypeStruct((1, 1, ATOMS), F32),
                jax.ShapeDtypeStruct((3, 1, ATOMS), F32),
            ),
            in_specs=[pl.BlockSpec(memory_space=pl.ANY)] * 17,
            out_specs=[pl.BlockSpec(memory_space=pltpu.VMEM)] * 2,
            scratch_shapes=[
                vmem(EXT, EDGES, dtype=BF16),
                vmem(1, EDGES, dtype=jnp.int32),
                vmem(3 * C, EDGES),
                vmem(4 * C, EDGES),
                vmem(C, EDGES),
                vmem(4 * C, EDGES),
                vmem(8 * C, EDGES, dtype=BF16),
                vmem(64, EDGES),
                vmem(64, EDGES),
                vmem(8, EDGES),
                vmem(8, EDGES),
                vmem(8, EDGES),
                vmem(8, EDGES),
                vmem(8, EDGES),
                vmem(1, EDGES),
                vmem(9 * C, ATOMS),
                vmem(9 * C, ATOMS),
                vmem(9 * C, ATOMS),
                vmem(8 * C, EXT, dtype=BF16),
                vmem(4 * C, BORDER),
                vmem(8, 4 * C, BORDER),
                vmem(10, 4 * C, BORDER),
                vmem(8, 4 * C, BORDER),
                vmem(8, BORDER),
                vmem(8, 8, BORDER),
                vmem(8, 8, BORDER),
                vmem(8, 8, BORDER),
                pltpu.SemaphoreType.DMA((5, 8)),
                pltpu.SemaphoreType.DMA((5, 8)),
                [vmem(*arg.shape, dtype=arg.dtype) for arg in args],
                pltpu.SemaphoreType.DMA((17,)),
            ],
            compiler_params=pltpu.CompilerParams(
                collective_id=0, has_side_effects=True, vmem_limit_bytes=63 * 2**20
            ),
        )(*args)
        return energies, forces.reshape(1, 1, 3, ATOMS)

    def specs():
        lead = [P("dom", "sub", None, None), P("dom", "sub", None)]
        return (lead[0], lead[1], lead[1], lead[0]) + (P(),) * 13

    return jax.shard_map(
        body,
        mesh=mesh,
        in_specs=specs(),
        out_specs=(P("dom", "sub", None), P("dom", "sub", None, None)),
        check_vma=False,
    )
```

```python
import math

import jax
import jax.numpy as jnp
from jax import lax
from jax.experimental import pallas as pl
from jax.experimental.pallas import tpu as pltpu
from jax.sharding import PartitionSpec as P

CUTOFF = 5.0
MESH = pl.DeviceIdType.MESH
F32 = jnp.float32
BF16 = jnp.bfloat16
C = 128
SLOTS = 16
ATOMS = 256
BORDER = 128
EDGES = SLOTS * ATOMS
EXT = ATOMS + 8 * BORDER
SIDES = [(0, -1), (0, 1), (-1, 0), (1, 0), (-1, 1), (1, 1), (-1, -1), (1, -1)]
HALF = SLOTS ** (-0.5)


def dot(a, b):
    return jnp.dot(a, b, preferred_element_type=F32)


def dot_nt(a, b):
    return lax.dot_general(a, b, (((1,), (1,)), ((), ())), preferred_element_type=F32)


def split(x):
    high = x.astype(BF16)
    return high, (x - high.astype(F32)).astype(BF16)


def stack2(x):
    high = x.astype(BF16).astype(F32)
    return jnp.concatenate([high, x - high], axis=0).astype(BF16)


def stack4(x):
    high = x.astype(BF16).astype(F32)
    rest = x - high
    mid = rest.astype(BF16).astype(F32)
    return jnp.concatenate([high, mid, rest - mid, jnp.zeros_like(x)], axis=0).astype(BF16)


def turned(weight, copies=1):
    tall = weight.astype(F32)
    if copies > 1:
        tall = jnp.concatenate([tall] * copies, axis=0)
    return tall.T.astype(BF16)


def doubled(weight):
    return jnp.concatenate([weight, weight], axis=1)


def sine(z):
    z2 = z * z
    out = 1.0 / 6227020800.0
    for coefficient in (-1.0 / 39916800.0, 1.0 / 362880.0, -1.0 / 5040.0, 1.0 / 120.0, -1.0 / 6.0, 1.0):
        out = out * z2 + coefficient
    return out * z


def cosine(z):
    z2 = z * z
    out = 1.0 / 479001600.0 - z2 * (1.0 / 87178291200.0)
    for coefficient in (-1.0 / 3628800.0, 1.0 / 40320.0, -1.0 / 720.0, 1.0 / 24.0, -0.5, 1.0):
        out = out * z2 + coefficient
    return out


def sigmoid(x):
    return 1.0 / (1.0 + jnp.exp(-x))


def lanes(k, width=ATOMS):
    return pl.ds(pl.multiple_of(k * width, width), width)


def kernel(
    shape_of_mesh,
    inputs,
    energy_ref,
    force_ref,
    hot,
    listed,
    rad1,
    rad2,
    src1,
    src2,
    terms,
    slope1,
    slope2,
    basis,
    basis_slope,
    shift,
    harm,
    d_harm,
    d_radius,
    amps1,
    amps2,
    back,
    feats,
    out_feat,
    got_feat,
    out_grad,
    got_grad,
    out_pos,
    got_pos,
    out_force,
    got_force,
    send_sem,
    recv_sem,
    fetched,
    fetch_sem,
):
    n_dom, n_sub = shape_of_mesh
    dom = lax.axis_index("dom")
    sub = lax.axis_index("sub")

    toward = 1 - 2 * lax.rem(sub, 2)

    def device(a, b):
        return (lax.rem(dom + a + n_dom, n_dom), lax.rem(sub + b * toward + n_sub, n_sub))

    barrier = pltpu.get_barrier_semaphore()
    for a, b in SIDES:
        pl.semaphore_signal(barrier, inc=1, device_id=device(a, b), device_id_type=MESH)

    fetches = [
        pltpu.make_async_copy(source, target, fetch_sem.at[n])
        for n, (source, target) in enumerate(zip(inputs, fetched))
    ]
    for copy in fetches:
        copy.start()
    (
        pos_ref,
        spec_ref,
        bound_ref,
        neigh_ref,
        embed_ref,
        rad1_in_ref,
        rad1_out_ref,
        self1_ref,
        mix1_ref,
        gate1_ref,
        read1_ref,
        rad2_in_ref,
        rad2_out_ref,
        self2_ref,
        mix2_ref,
        out_in_ref,
        out_last_ref,
    ) = fetched

    def transfer(phase, source, target, o, side):
        return pltpu.make_async_remote_copy(
            src_ref=source,
            dst_ref=target,
            send_sem=send_sem.at[phase, o],
            recv_sem=recv_sem.at[phase, o],
            device_id=device(*side),
            device_id_type=MESH,
        )

    for copy in fetches[:4]:
        copy.wait()

    own_rows = jnp.concatenate(
        [pos_ref[:, 0, :], spec_ref[0].astype(F32), jnp.zeros((4, ATOMS), F32)], axis=0
    )
    border_hot = (
        lax.broadcasted_iota(jnp.int32, (ATOMS, BORDER), 0) == bound_ref[0]
    ).astype(F32).astype(BF16)
    picked = dot(stack4(own_rows), border_hot)
    out_pos[...] = picked[0:8] + picked[8:16] + picked[16:24]

    entries = neigh_ref[0, 0]
    number = lax.shift_right_logical(entries, 7)
    place = jnp.where(number < 2, number, EXT // BORDER)
    for o, (a, b) in enumerate(SIDES):
        place = jnp.where(number == 6 + 3 * a + b * toward, 2 + o, place)
    entries = place * BORDER + (entries & (BORDER - 1))
    for k in range(SLOTS):
        listed[:, k * ATOMS : (k + 1) * ATOMS] = entries[k : k + 1]

    def build(k, carry):
        at = lanes(k)
        ids = lax.broadcasted_iota(jnp.int32, (EXT, ATOMS), 0)
        hot[:, at] = jnp.where(ids == listed[:, at], 1.0, 0.0).astype(BF16)
        return carry

    lax.fori_loop(0, SLOTS // 2, build, 0)
    pl.semaphore_wait(barrier, 8)
    sent_pos = [transfer(0, out_pos, got_pos.at[o], o, (-a, b)) for o, (a, b) in enumerate(SIDES)]
    for copy in sent_pos:
        copy.start()
    lax.fori_loop(SLOTS // 2, SLOTS, build, 0)
    for copy in fetches[4:]:
        copy.wait()

    self1_t = turned(self1_ref[...])
    mix1_t = turned(mix1_ref[...], 2)
    gate1_t = turned(gate1_ref[...], 2)
    self2_t = turned(self2_ref[...], 2)
    mix2_t = turned(mix2_ref[...], 2)
    out_in_wide = turned(out_in_ref[...])
    read = jnp.concatenate([jnp.broadcast_to(read1_ref[...], (C, C)).T] * 2, axis=1)
    last = jnp.concatenate([jnp.broadcast_to(out_last_ref[...], (C, 16)).T] * 2, axis=1)
    rad1_in_t = turned(rad1_in_ref[...], 2)
    rad1_out_t = turned(rad1_out_ref[...], 2)
    rad2_in_t = turned(rad2_in_ref[...], 2)
    rad2_out_t = turned(rad2_out_ref[...], 2)
    embed_t = turned(
        jnp.concatenate([embed_ref[...].astype(F32), jnp.zeros((6, C), F32)], axis=0)
    )

    for copy in sent_pos:
        copy.wait()
    blocks = [own_rows[0:4, 0:BORDER], own_rows[0:4, BORDER:]] + [got_pos[o][0:4] for o in range(8)]
    table = [jnp.concatenate(blocks[n : n + 2], axis=0) for n in range(0, 10, 2)]

    def geometry(g, carry):
        at = lanes(g, 1024)
        there = []
        for part in range(8):
            ids = listed[:, pl.ds(pl.multiple_of(g * 1024 + part * 128, 128), 128)]
            ids = jnp.broadcast_to(ids, (8, 128))
            inside = ids & (BORDER - 1)
            block = lax.shift_right_logical(ids, 7)
            found = jnp.zeros((8, 128), F32)
            for n in range(5):
                taken = jnp.take_along_axis(table[n], inside, axis=1, mode="promise_in_bounds")
                found = jnp.where(lax.shift_right_logical(block, 1) == n, taken, found)
            there.append(jnp.where((block & 1)[0:4] == 1, found[4:8], found[0:4]))
        there = jnp.concatenate(there, axis=1)
        here = jnp.concatenate([own_rows[0:4]] * 4, axis=1)
        u = (there - here) * (1.0 / CUTOFF)
        shift[0:4, at] = u
        ux, uy, uz = u[0:1], u[1:2], u[2:3]
        r2 = ux * ux + uy * uy + uz * uz
        present = jnp.where(listed[:, at] < EXT, 1.0, 0.0)
        room = jnp.maximum(1.0 - r2, 0.0) * present
        orders = lax.broadcasted_iota(jnp.int32, (8, 1024), 0).astype(F32)
        turns = orders * jnp.minimum(r2, 1.0)
        turns = turns - 2.0 * jnp.floor(0.5 * turns + 0.5)
        z = (0.5 * math.pi) * turns
        sz, cz = sine(z), cosine(z)
        cos_n = 1.0 - 2.0 * sz * sz
        sin_n = 2.0 * sz * cz
        envelope = room * room
        base = envelope * cos_n
        basis[:, at] = base
        basis_slope[:, at] = -2.0 * room * cos_n - (math.pi * orders) * (envelope * sin_n)
        harm[0:1, at] = 1.7 * ux
        harm[1:2, at] = 1.7 * uy
        harm[2:3, at] = 1.7 * uz
        harm[3:4, at] = 3.9 * ux * uy
        harm[4:5, at] = 3.9 * uy * uz
        harm[5:6, at] = 1.1 * (3.0 * uz * uz - r2)
        harm[6:7, at] = 3.9 * ux * uz
        harm[7:8, at] = 1.95 * (ux * ux - uy * uy)
        kinds = lax.broadcasted_iota(jnp.int32, (16, 1024), 0).astype(F32)
        src1[:, at] = dot(embed_t, jnp.where(kinds == there[3:4], 1.0, 0.0).astype(BF16))
        radial(base, rad1_in_t, rad1_out_t, slope1, rad1, at)
        return carry

    def radial(base, in_t, out_t, slope, rad, at):
        pre = dot(in_t, stack2(base))
        gate = sigmoid(pre)
        slope[:, at] = gate * (1.0 + pre * (1.0 - gate))
        rad[:, at] = dot(out_t, stack2(pre * gate))

    lax.fori_loop(0, 4, geometry, 0)

    def aggregate(rad, src, amps, vectors):
        def step(t, carry):
            r = t * 8
            total = [jnp.zeros((8, ATOMS), F32) for _ in range(9)]
            for k in range(SLOTS):
                at = slice(k * ATOMS, (k + 1) * ATOMS)

                def rows(ref, block):
                    return ref[pl.ds(pl.multiple_of(block * C + r, 8), 8), at]

                s = rows(src, 0)
                total[0] += rows(rad, 0) * s
                p1 = rows(rad, 1) * s
                p2 = rows(rad, 2) * s
                for m in range(3):
                    total[1 + m] += p1 * harm[m : m + 1, at]
                for m in range(3, 8):
                    total[1 + m] += p2 * harm[m : m + 1, at]
                if vectors:
                    r3 = rows(rad, 3)
                    for m in range(3):
                        total[1 + m] += r3 * rows(src, 1 + m)
            for m in range(9):
                amps[pl.ds(pl.multiple_of(m * C + r, 8), 8), :] = total[m] * HALF
            return carry

        lax.fori_loop(0, C // 8, step, 0)

    def invariants(amps):
        a = [amps[m * C : (m + 1) * C, :] for m in range(9)]
        dipole = a[1] * a[1] + a[2] * a[2] + a[3] * a[3]
        quadrupole = a[4] * a[4] + a[5] * a[5] + a[6] * a[6] + a[7] * a[7] + a[8] * a[8]
        return jnp.concatenate([a[0], dipole, quadrupole], axis=0)

    aggregate(rad1, src1, amps1, False)
    own_kinds = lax.broadcasted_iota(jnp.int32, (16, ATOMS), 0)
    own_node = dot(embed_t, jnp.where(own_kinds == spec_ref[0], 1.0, 0.0).astype(BF16))
    scalars = dot(self1_t, own_node.astype(BF16)) + dot(
        mix1_t, stack2(invariants(amps1))
    )
    gating = sigmoid(dot(gate1_t, stack2(scalars)))
    energy_one = jnp.sum(read * scalars, axis=0, keepdims=True)
    own_feat = jnp.concatenate(
        [scalars] + [amps1[m * C : (m + 1) * C, :] * gating for m in range(1, 4)], axis=0
    )
    for half in range(2):
        feats[half * 512 : half * 512 + 512, 0:ATOMS] = stack2(
            own_feat[half * 256 : half * 256 + 256]
        )
    picked_feat = dot(feats[:, 0:ATOMS], border_hot)
    for half in range(2):
        at = half * 512
        out_feat[half * 256 : half * 256 + 256] = (
            picked_feat[at : at + 256] + picked_feat[at + 256 : at + 512]
        )
    def feature_way(half, source, o, side):
        rows = pl.ds(half * 256, 256)
        return transfer(1 + 3 * half, source.at[rows], got_feat.at[o, rows], o, side)

    sent_feat = [
        [
            feature_way(half, out_feat, 0, (0, -1)),
            feature_way(half, out_feat, 1, (0, 1)),
            feature_way(half, out_feat, 2, (1, 0)),
            feature_way(half, out_feat, 3, (-1, 0)),
            feature_way(half, got_feat.at[2], 4, (0, 1)),
            feature_way(half, got_feat.at[3], 5, (0, 1)),
            feature_way(half, got_feat.at[0], 6, (1, 0)),
            feature_way(half, got_feat.at[0], 7, (-1, 0)),
        ]
        for half in range(2)
    ]
    for half in range(2):
        for o in (0, 2, 3, 1):
            sent_feat[half][o].start()

    def second_radial(g, carry):
        at = lanes(g, 1024)
        radial(basis[:, at], rad2_in_t, rad2_out_t, slope2, rad2, at)
        return carry

    lax.fori_loop(0, 4, second_radial, 0)

    self_part = dot(self2_t, stack2(scalars))

    def gather(tiles, halves):
        def step(g, carry):
            at = lanes(g, 1024)
            rows = slice(halves[0] * 512, halves[-1] * 512 + 512)
            cols = slice(tiles[0] * 256, tiles[-1] * 256 + 256)
            found = dot(feats[rows, cols], hot[cols, at])
            for n, half in enumerate(halves):
                to = slice(half * 256, half * 256 + 256)
                value = found[n * 512 : n * 512 + 256] + found[n * 512 + 256 : n * 512 + 512]
                src2[to, at] = value if tiles[0] == 0 else src2[to, at] + value
            return carry

        lax.fori_loop(0, 4, step, 0)

    def arrived(tile, half):
        for o in (2 * tile - 2, 2 * tile - 1):
            feats[half * 512 : half * 512 + 512, ATOMS + o * BORDER : ATOMS + (o + 1) * BORDER] = (
                stack2(got_feat[o, half * 256 : half * 256 + 256])
            )

    gather((0,), (0, 1))
    for half in range(2):
        for o, relayed in ((0, (6, 7)), (2, (4,)), (3, (5,))):
            sent_feat[half][o].wait_recv()
            for later in relayed:
                sent_feat[half][later].start()
        sent_feat[half][1].wait_recv()
        for tile in (1, 2):
            arrived(tile, half)
        gather((1, 2), (half,))
    for tile in (3, 4):
        for half in range(2):
            for o in (2 * tile - 2, 2 * tile - 1):
                sent_feat[half][o].wait_recv()
            arrived(tile, half)
        gather((tile,), (0, 1))
    for half in range(2):
        for copy in sent_feat[half]:
            copy.wait_send()
    aggregate(rad2, src2, amps2, True)
    scalars_two = self_part + dot(mix2_t, stack2(invariants(amps2)))
    pre = dot(doubled(out_in_ref[...]), stack2(scalars_two))
    gate = sigmoid(pre)
    energy_two = jnp.sum(last * (pre * gate), axis=0, keepdims=True)
    energy_ref[0] = energy_one + energy_two

    d_pre = last * (gate * (1.0 + pre * (1.0 - gate)))
    d_pre_high, d_pre_low = split(d_pre)
    d_two = dot(out_in_wide, d_pre_high) + dot(out_in_wide, d_pre_low)
    d_two_terms = stack2(d_two)
    d_self = dot(doubled(self2_ref[...]), d_two_terms)
    d_inv = dot(doubled(mix2_ref[...]), d_two_terms)

    def to_back(amps, d_inv, extra):
        back[0:C, :] = d_inv[0:C] * HALF
        for m in range(1, 9):
            block = d_inv[C : 2 * C] if m < 4 else d_inv[2 * C : 3 * C]
            value = 2.0 * amps[m * C : (m + 1) * C, :] * block
            if extra is not None and m < 4:
                value = value + extra[m - 1]
            back[m * C : (m + 1) * C, :] = value * HALF

    to_back(amps2, d_inv, None)

    def source_grads(k, carry):
        at = lanes(k)
        for t in range(C // 16):
            b = [back[m * C + t * 16 : m * C + t * 16 + 16, :] for m in range(9)]
            r0, r1, r2, r3 = [rad2[l * C + t * 16 : l * C + t * 16 + 16, at] for l in range(4)]
            t1 = harm[0:1, at] * b[1] + harm[1:2, at] * b[2] + harm[2:3, at] * b[3]
            t2 = harm[3:4, at] * b[4]
            for m in range(4, 8):
                t2 = t2 + harm[m : m + 1, at] * b[m + 1]
            grads = [r0 * b[0] + r1 * t1 + r2 * t2] + [r3 * b[m] for m in range(1, 4)]
            for l in range(4):
                high, low = split(grads[l])
                terms[l * C + t * 16 : l * C + t * 16 + 16, at] = high
                terms[512 + l * C + t * 16 : 512 + l * C + t * 16 + 16, at] = low
        return carry

    lax.fori_loop(0, SLOTS, source_grads, 0)

    sent_grad = [
        transfer(2, out_grad.at[2], got_grad.at[0], 0, (0, -1)),
        transfer(2, out_grad.at[3], got_grad.at[1], 1, (0, 1)),
        transfer(2, out_grad.at[4], got_grad.at[2], 2, (-1, 0)),
        transfer(2, out_grad.at[5], got_grad.at[3], 3, (1, 0)),
        transfer(2, out_grad.at[6], got_grad.at[4], 4, (0, 1)),
        transfer(2, out_grad.at[7], got_grad.at[5], 5, (0, 1)),
        transfer(2, out_grad.at[8], got_grad.at[6], 6, (-1, 0)),
        transfer(2, out_grad.at[9], got_grad.at[7], 7, (1, 0)),
    ]

    def scatter(n, carry):
        tile = 4 - n
        summed = dot_nt(terms[...], hot[lanes(tile), :])
        summed = summed[0:512] + summed[512:1024]
        out_grad[2 * tile] = summed[:, 0:BORDER]
        out_grad[2 * tile + 1] = summed[:, BORDER : 2 * BORDER]

        @pl.when(n == 0)
        def _():
            sent_grad[6].start()
            sent_grad[7].start()

        @pl.when(n == 1)
        def _():
            sent_grad[4].start()
            sent_grad[5].start()

        @pl.when(n == 2)
        def _():
            for o in (2, 3):
                sent_grad[2 + o].wait_recv()
                out_grad[2 + o] = out_grad[2 + o] + got_grad[2 + o]
                sent_grad[o].start()

        @pl.when(n == 3)
        def _():
            sent_grad[1].start()
            sent_grad[6].wait_recv()
            sent_grad[7].wait_recv()
            out_grad[2] = out_grad[2] + got_grad[6] + got_grad[7]
            sent_grad[0].start()

        return carry

    lax.fori_loop(0, 5, scatter, 0)

    def radial_grads(rad, src, slope, in_ref, out_ref, blocks, first):
        out_pair = doubled(out_ref[...])

        def step(k, carry):
            at = lanes(k)
            total = [jnp.zeros((8, ATOMS), F32) for _ in range(8)]
            for t in range(C // 16):
                b = [back[m * C + t * 16 : m * C + t * 16 + 16, :] for m in range(9)]
                t1 = harm[0:1, at] * b[1] + harm[1:2, at] * b[2] + harm[2:3, at] * b[3]
                t2 = harm[3:4, at] * b[4]
                for m in range(4, 8):
                    t2 = t2 + harm[m : m + 1, at] * b[m + 1]
                s = src[t * 16 : t * 16 + 16, at]
                grads = [s * b[0], s * t1, s * t2]
                if blocks == 4:
                    v = [src[l * C + t * 16 : l * C + t * 16 + 16, at] for l in range(1, 4)]
                    grads.append(v[0] * b[1] + v[1] * b[2] + v[2] * b[3])
                for l in range(blocks):
                    high, low = split(grads[l])
                    terms[l * C + t * 16 : l * C + t * 16 + 16, at] = high
                    terms[
                        (blocks + l) * C + t * 16 : (blocks + l) * C + t * 16 + 16, at
                    ] = low
                p1 = rad[C + t * 16 : C + t * 16 + 16, at] * s
                p2 = rad[2 * C + t * 16 : 2 * C + t * 16 + 16, at] * s
                for m in range(8):
                    product = (p1 if m < 3 else p2) * b[m + 1]
                    total[m] += product[0:8] + product[8:16]
            for m in range(8):
                value = jnp.sum(total[m], axis=0, keepdims=True)
                if not first:
                    value = value + d_harm[m : m + 1, at]
                d_harm[m : m + 1, at] = value
            return carry

        lax.fori_loop(0, SLOTS, step, 0)

        def tail(g, carry):
            at = lanes(g, 2048)
            d_hidden = dot(out_pair, terms[0 : 2 * blocks * C, at]) * slope[:, at]
            high, low = split(d_hidden)
            d_basis = dot(in_ref[...], high) + dot(in_ref[...], low)
            value = jnp.sum(d_basis * basis_slope[:, at], axis=0, keepdims=True)
            if not first:
                value = value + d_radius[:, at]
            d_radius[:, at] = value
            return carry

        lax.fori_loop(0, 2, tail, 0)

    radial_grads(rad2, src2, slope2, rad2_in_ref, rad2_out_ref, 4, True)

    for copy in sent_grad[:4]:
        copy.wait_recv()
    for copy in sent_grad:
        copy.wait_send()
    returned = got_grad[0]
    for o in range(1, 4):
        returned = returned + got_grad[o]
    placed = dot_nt(stack2(returned), border_hot)
    d_feat = jnp.concatenate([out_grad[0], out_grad[1]], axis=1) + placed[0:512] + placed[512:1024]
    d_vec = [d_feat[m * C : (m + 1) * C] for m in range(1, 4)]
    d_gate = (
        d_vec[0] * amps1[C : 2 * C, :]
        + d_vec[1] * amps1[2 * C : 3 * C, :]
        + d_vec[2] * amps1[3 * C : 4 * C, :]
    ) * (gating * (1.0 - gating))
    d_scalars = d_feat[0:C] + d_self + read + dot(doubled(gate1_ref[...]), stack2(d_gate))
    d_inv_one = dot(doubled(mix1_ref[...]), stack2(d_scalars))
    to_back(amps1, d_inv_one, [d * gating for d in d_vec])
    radial_grads(rad1, src1, slope1, rad1_in_ref, rad1_out_ref, 3, False)

    def to_shift(g, carry):
        at = lanes(g, 1024)
        ux, uy, uz = [shift[m : m + 1, at] for m in range(3)]
        d = [d_harm[m : m + 1, at] for m in range(8)]
        dr = 2.0 * (d_radius[:, at] - 1.1 * d[5])
        basis[0:1, at] = (
            1.7 * d[0] + 3.9 * (uy * d[3] + uz * d[6] + ux * d[7]) + ux * dr
        ) * (1.0 / CUTOFF)
        basis[1:2, at] = (
            1.7 * d[1] + 3.9 * (ux * d[3] + uz * d[4] - uy * d[7]) + uy * dr
        ) * (1.0 / CUTOFF)
        basis[2:3, at] = (
            1.7 * d[2] + 3.9 * (uy * d[4] + ux * d[6]) + uz * (6.6 * d[5] + dr)
        ) * (1.0 / CUTOFF)
        basis[3:8, at] = jnp.zeros((5, 1024), F32)
        return carry

    lax.fori_loop(0, 4, to_shift, 0)
    d_edges = stack4(basis[...])
    sent_force = [
        transfer(3, out_force.at[o], got_force.at[o], o, side) for o, side in enumerate(SIDES)
    ]
    for n in (4, 3, 2, 1, 0):
        summed = dot_nt(d_edges, hot[n * 256 : (n + 1) * 256, :])
        summed = summed[0:8] + summed[8:16] + summed[16:24]
        if n > 0:
            for o in (2 * n - 2, 2 * n - 1):
                out_force[o] = summed[:, (o % 2) * BORDER : (o % 2 + 1) * BORDER]
                sent_force[o].start()
    own_force = summed
    for k in range(SLOTS):
        own_force = own_force - basis[:, k * ATOMS : (k + 1) * ATOMS]
    for copy in sent_force:
        copy.wait()
    returned = got_force[0]
    for o in range(1, 8):
        returned = returned + got_force[o]
    placed = dot_nt(stack4(returned), border_hot)
    own_force = own_force + placed[0:8] + placed[8:16] + placed[16:24]
    for m in range(3):
        force_ref[m] = -own_force[m : m + 1]


def solution(mesh):
    shape_of_mesh = (mesh.shape["dom"], mesh.shape["sub"])

    def vmem(*shape, dtype=F32):
        return pltpu.VMEM(shape, dtype)

    def body(*args):
        args = list(args)
        args[0] = args[0].reshape(3, 1, ATOMS)
        args[10] = args[10].reshape(1, C)
        args[15] = args[15].T
        args[16] = args[16].reshape(1, 16)

        def run(*refs):
            kernel(shape_of_mesh, refs[:17], *refs[17:-2], refs[-2], refs[-1])

        energies, forces = pl.pallas_call(
            run,
            out_shape=(
                jax.ShapeDtypeStruct((1, 1, ATOMS), F32),
                jax.ShapeDtypeStruct((3, 1, ATOMS), F32),
            ),
            in_specs=[pl.BlockSpec(memory_space=pl.ANY)] * 17,
            out_specs=[pl.BlockSpec(memory_space=pltpu.VMEM)] * 2,
            scratch_shapes=[
                vmem(EXT, EDGES, dtype=BF16),
                vmem(1, EDGES, dtype=jnp.int32),
                vmem(3 * C, EDGES),
                vmem(4 * C, EDGES),
                vmem(C, EDGES),
                vmem(4 * C, EDGES),
                vmem(8 * C, EDGES, dtype=BF16),
                vmem(64, EDGES),
                vmem(64, EDGES),
                vmem(8, EDGES),
                vmem(8, EDGES),
                vmem(8, EDGES),
                vmem(8, EDGES),
                vmem(8, EDGES),
                vmem(1, EDGES),
                vmem(9 * C, ATOMS),
                vmem(9 * C, ATOMS),
                vmem(9 * C, ATOMS),
                vmem(8 * C, EXT, dtype=BF16),
                vmem(4 * C, BORDER),
                vmem(8, 4 * C, BORDER),
                vmem(10, 4 * C, BORDER),
                vmem(8, 4 * C, BORDER),
                vmem(8, BORDER),
                vmem(8, 8, BORDER),
                vmem(8, 8, BORDER),
                vmem(8, 8, BORDER),
                pltpu.SemaphoreType.DMA((5, 8)),
                pltpu.SemaphoreType.DMA((5, 8)),
                [vmem(*arg.shape, dtype=arg.dtype) for arg in args],
                pltpu.SemaphoreType.DMA((17,)),
            ],
            compiler_params=pltpu.CompilerParams(
                collective_id=0, has_side_effects=True, vmem_limit_bytes=63 * 2**20
            ),
        )(*args)
        return energies, forces.reshape(1, 1, 3, ATOMS)

    def specs():
        lead = [P("dom", "sub", None, None), P("dom", "sub", None)]
        return (lead[0], lead[1], lead[1], lead[0]) + (P(),) * 13

    return jax.shard_map(
        body,
        mesh=mesh,
        in_specs=specs(),
        out_specs=(P("dom", "sub", None), P("dom", "sub", None, None)),
        check_vma=False,
    )
```
